128 devices in a mesh: section: 16 (over y_hi, x, core), tp: 8 (over y_lo, z).
Axes of the slice: x: 4, y: 4 (y_hi: 2, y_lo: 2; y = y_hi * 2 + y_lo), z: 4, core: 2. Of those that a mesh axis runs over, the one named last changes fastest.
Arguments:
- activations: bfloat16 [16, 5, 1024, 8192], P('section', None, None, 'tp'), may hold values from -6 to 6
- cotangents: bfloat16 [16, 5, 1024, 2048], P('section', None, None, 'tp'), may hold values from -0.3984375 to 0.3984375
- section_code: int32 [16], replicated, may hold values from 0 to 15, each once
- boundaries: int32 [3, 17], replicated, may hold values from 0 to 16, as said below
- micro_counts: int32 [3], replicated, may hold values from 1 to 4, as said below
Outputs:
- layer_grads: float32 [16, 8192, 2048], P(None, 'tp', 'section')
The draws below stay inside these ranges and needn't reach their ends.
Inputs may be any that keep to these rules, and one draw needn't show every extreme that they name: Row r lists replica r's boundaries: 0, then rising sums of its sections' lengths (4, 5, 7 sections), each 1 to 5 layers, ending at 16, then 16 repeated to the row's end; every replica has a section of exactly 5 layers. `micro_counts`: some replica has exactly 4.
All inputs are finite; a program needn't handle non-finite values.
Results may differ from the reference program's by a relative error of at most 0.0029.
Values may be sent and summed in bfloat16 or wider, within the bound.
A program may use at most 192 MiB of HBM per device.

```python
import jax
import jax.numpy as jnp
from jax import lax

D = 8192
KVC = 2048
MBT = 256
MB_MAX = 4
ROWS = 1024
MAXL = 5
LAYERS = 16
REP_A = 4
REP_B = 5
REP_C = 7
N_SECTION = 16


def section_lengths(base_key, section_count):
    lengths = jnp.ones((section_count,), jnp.int32)
    picked = jax.random.randint(jax.random.fold_in(base_key, 0), (), 0, section_count)
    lengths = jnp.where(jnp.arange(section_count) == picked, MAXL, lengths).astype(jnp.int32)
    for extra_step in range(LAYERS - MAXL - (section_count - 1)):
        scores = jax.random.randint(jax.random.fold_in(base_key, extra_step + 1), (section_count,), 0, 1 << 20)
        scores = jnp.where(lengths < MAXL, scores, -1)
        chosen = jnp.argmax(scores)
        lengths = lengths + (jnp.arange(section_count) == chosen).astype(jnp.int32)
    return lengths


def draw_boundaries(key, part):
    key = jax.random.fold_in(key, 11)
    bound_rows = []
    for replica, section_count in enumerate((REP_A, REP_B, REP_C)):
        lengths = section_lengths(jax.random.fold_in(key, replica), section_count)
        section_ends = jnp.cumsum(lengths).astype(jnp.int32)
        bound_row = jnp.concatenate([jnp.zeros((1,), jnp.int32), section_ends, jnp.full((N_SECTION - section_count,), LAYERS, jnp.int32)])
        bound_rows.append(bound_row)
    return jnp.stack(bound_rows).astype(jnp.int32)


def draw_micro_counts(key, part):
    key = jax.random.fold_in(key, 23)
    drawn = jax.random.randint(jax.random.fold_in(key, 1), (3,), 1, MB_MAX + 1)
    fullest = jax.random.randint(jax.random.fold_in(key, 2), (), 0, 3)
    return jnp.where(jnp.arange(3) == fullest, MB_MAX, drawn).astype(jnp.int32)


def block_levels(own_key, shape, cuts, least, high):
    factor_of, own = 1.0, jax.random.fold_in(own_key, 6)
    for axis_at, parts in cuts:
        heights = jnp.exp(jax.random.uniform(jax.random.fold_in(own, axis_at), (parts,), jnp.float32, least / len(cuts), high / len(cuts)))
        factor_of = factor_of * jnp.repeat(heights, shape[axis_at] // parts).reshape([-1 if axis == axis_at else 1 for axis in range(len(shape))])
    return factor_of


def noise(key, extent, scale, most, cuts=(), kind=jnp.bfloat16):
    entries = scale * jax.random.normal(key, extent, jnp.float32)
    if cuts:
        entries = entries * block_levels(key, extent, cuts, -0.22, 0.18)
    return jnp.clip(entries, -most, most).astype(kind)


def setup_inputs(seed: int = 0) -> dict:
    keys = jax.random.split(jax.random.key(seed), 6)
    return {
        "activations": noise(keys[0], (N_SECTION, MAXL, ROWS, D), 1.0, 6.0, ((0, 16), (3, 8))),
        "cotangents": noise(keys[1], (N_SECTION, MAXL, ROWS, KVC), 0.05, 0.3984375, ((0, 16), (3, 8))),
        "section_code": jax.random.permutation(keys[2], N_SECTION).astype(jnp.int32),
        "boundaries": draw_boundaries(jax.random.fold_in(keys[5], 71), 0),
        "micro_counts": draw_micro_counts(jax.random.fold_in(keys[5], 71), 0),
    }


def reference(activations, cotangents, section_code, boundaries, micro_counts):
    start_second = N_SECTION // 4
    start_third = start_second + (5 * N_SECTION) // 16
    first_codes = [0, start_second, start_third]
    row_index = jnp.arange(ROWS, dtype=jnp.int32)
    layer_grads = jnp.zeros((LAYERS, D, KVC), jnp.float32)
    for replica in range(3):
        row_limit = MBT * micro_counts[replica]
        live_rows = (row_index < row_limit)[:, None]

        def add_layer(layer, totals, replica=replica, live_rows=live_rows):
            section_index = jnp.sum((boundaries[replica, 1:] <= layer).astype(jnp.int32)).astype(jnp.int32)
            wanted = (first_codes[replica] + section_index).astype(jnp.int32)
            holder = jnp.argmax((section_code == wanted).astype(jnp.int32)).astype(jnp.int32)
            slot_index = (layer - boundaries[replica, section_index]).astype(jnp.int32)
            inputs = activations[holder, slot_index]
            grads_in = cotangents[holder, slot_index]
            masked = jnp.where(live_rows, grads_in, jnp.zeros((), grads_in.dtype))
            grad_block = jnp.dot(inputs.T, masked, preferred_element_type=jnp.float32).astype(jnp.bfloat16)
            return totals.at[layer].add(grad_block.astype(jnp.float32))

        layer_grads = lax.fori_loop(0, LAYERS, add_layer, layer_grads)
    return layer_grads
```

```python
import functools

import jax
import jax.numpy as jnp
from jax import lax
from jax.experimental import pallas as pl
from jax.experimental.pallas import tpu as pltpu
from jax.sharding import PartitionSpec as P

MBT = 256
MESH = pl.DeviceIdType.MESH
SLOTS = 5
UNITS = 2 * SLOTS
ROWS = 1024
WIDTH = 1024
LAYERS = 16
CHUNKS = 8
CROWS = 512 // CHUNKS


def place():
    section = lax.axis_index("section")
    tp = lax.axis_index("tp")
    return section // 8, (section // 2) % 4, section % 2, tp // 4, tp % 4


def device(yh, x, c, yl, z):
    return ((yh * 4 + x) * 2 + c, yl * 4 + z)


def greet(peers):
    barrier = pltpu.get_barrier_semaphore()
    for peer in peers:
        pl.semaphore_signal(barrier, inc=1, device_id=peer, device_id_type=MESH)
    pl.semaphore_wait(barrier, len(peers))


def gather_multiply(
    c_ref, a_ref, kept, recv, a2, cbuf, abuf, stk, sts,
    loc_sem, cs_sem, cr_sem, as_sem, ar_sem, ms_sem, mr_sem, al_sem, k_sem, ps_sem, pr_sem,
):
    yh, x, c, yl, z = place()
    xa = x + 1 - 2 * (x % 2)
    xb = 3 - x
    mate = device(yh, x, 1 - c, yl, z)
    ypeer = device(yh, x, c, 1 - yl, z)
    zplus = device(yh, x, c, yl, (z + 1) % 4)
    zminus = device(yh, x, c, yl, (z + 3) % 4)
    peer_a = device(yh, xa, c, yl, z)
    peer_b = device(yh, xb, c, yl, z)
    greet((mate, ypeer, zplus, zminus, peer_a, peer_b))
    turn = 1 + 2 * (x % 2)

    def column(yy, zz):
        place_x = ((zz % 4 - x + 4) * turn) % 4
        place_y = (yy - yh + 2) % 2
        return pl.multiple_of((place_x * 2 + place_y) * 128, 128)

    def shard(s, yy, zz, row=0, rows=ROWS):
        return cbuf.at[s, pl.ds(row, rows), pl.ds(column(yy, zz), 128)]

    def own_c(j):
        return pltpu.make_async_copy(
            c_ref.at[j, :, pl.ds(pl.multiple_of(c * 128, 128), 128)], shard(2 * j, yl, z), loc_sem.at[j]
        )

    def mate_c(j):
        return pltpu.make_async_remote_copy(
            c_ref.at[j, :, pl.ds(pl.multiple_of((1 - c) * 128, 128), 128)],
            shard(2 * j + 1, yl, z), cs_sem.at[j], cr_sem.at[j], device_id=mate, device_id_type=MESH,
        )

    def mate_a(j):
        return pltpu.make_async_remote_copy(
            a_ref.at[j], a2.at[j], as_sem.at[j], ar_sem.at[j], device_id=mate, device_id_type=MESH
        )

    half = ROWS // 2

    def message(kind, s):
        if kind <= 2:
            ref, target = shard(s, yl, z), (ypeer, zplus, zminus)[kind]
        elif kind <= 4:
            ref, target = shard(s, 1 - yl, z), (zplus, zminus)[kind - 3]
        elif kind == 5:
            ref, target = shard(s, yl, z + 3, 0, half), zplus
        elif kind == 6:
            ref, target = shard(s, yl, z + 1, half, half), zminus
        else:
            ref, target = shard(s, yl, z + 2), ypeer
        return pltpu.make_async_remote_copy(
            ref, ref, ms_sem.at[kind, s], mr_sem.at[kind, s], device_id=target, device_id_type=MESH
        )

    def load_own(j):
        return pltpu.make_async_copy(a_ref.at[j], abuf.at[0], al_sem.at[0])

    def load_mate(j):
        return pltpu.make_async_copy(a2.at[j], abuf.at[1], al_sem.at[1])

    def keep(s, b):
        return pltpu.make_async_copy(stk.at[b], kept.at[s], k_sem.at[b])

    def swap(s, b, h):
        return pltpu.make_async_remote_copy(
            sts.at[b, h], recv.at[s, h], ps_sem.at[b, h], pr_sem.at[s, h],
            device_id=(peer_a, peer_b)[h], device_id_type=MESH,
        )

    for j in range(SLOTS):
        own_c(j).start()
        mate_c(j).start()
    load_own(0).start()
    for j in range(SLOTS):
        mate_a(j).start()

    def compute(s, b):
        j = s // 2
        if b == 0:
            mate_a(j).wait_recv()
            load_mate(j).start()
            load_own(j).wait()
        else:
            @pl.when(j < SLOTS - 1)
            def _():
                load_own(j + 1).start()

            load_mate(j).wait()

        @pl.when(j > 0)
        def _():
            keep(s - 2, b).wait()
            swap(s - 2, b, 0).wait_send()
            swap(s - 2, b, 1).wait_send()

        for h in range(2):
            @pl.loop(0, 2)
            def _(tile):
                at = pl.multiple_of(tile * 256, 256)
                block = lax.dot_general(
                    abuf[b, :, pl.ds(h * 512 + at, 256)], cbuf[s],
                    (((0,), (0,)), ((), ())), preferred_element_type=jnp.float32,
                ).astype(jnp.bfloat16)
                rows = pl.ds(at, 256)
                if h == 0:
                    sts[b, 0, rows, :] = block[:, 256:768]
                    stk[b, 0, rows, 0:256] = block[:, 0:256]
                    stk[b, 0, rows, 256:512] = block[:, 768:1024]
                else:
                    sts[b, 1, rows, 0:256] = block[:, 768:1024]
                    sts[b, 1, rows, 256:512] = block[:, 512:768]
                    stk[b, 1, rows, :] = block[:, 0:512]

            swap(s, b, h).start()
        keep(s, b).start()

    @pl.loop(0, UNITS + 3)
    def _(it):
        @pl.when(it < UNITS)
        def _():
            @pl.when(it % 2 == 0)
            def _():
                own_c(it // 2).wait()

            @pl.when(it % 2 == 1)
            def _():
                mate_c(it // 2).wait_recv()

            for kind in (0, 1, 2):
                message(kind, it).start()

        @pl.when((it >= 1) & (it < UNITS + 1))
        def _():
            s = it - 1
            message(0, s).wait_recv()
            message(3, s).start()
            message(4, s).start()
            message(1, s).wait_recv()
            message(5, s).start()
            message(2, s).wait_recv()
            message(6, s).start()

        @pl.when((it >= 2) & (it < UNITS + 2))
        def _():
            s = it - 2
            message(5, s).wait_recv()
            message(6, s).wait_recv()
            message(7, s).start()

        @pl.when(it >= 3)
        def _():
            s = it - 3
            message(3, s).wait_recv()
            message(4, s).wait_recv()
            message(7, s).wait_recv()

            @pl.when(s % 2 == 0)
            def _():
                compute(s, 0)

            @pl.when(s % 2 == 1)
            def _():
                compute(s, 1)

    for b in range(2):
        s = UNITS - 2 + b
        keep(s, b).wait()
        swap(s, b, 0).wait_send()
        swap(s, b, 1).wait_send()
    for j in range(SLOTS):
        mate_c(j).wait_send()
        mate_a(j).wait_send()

    @pl.loop(0, UNITS)
    def _(s):
        for kind in range(8):
            message(kind, s).wait_send()
        for h in range(2):
            swap(s, 0, h).wait_recv()


def merge(
    slot_of, weight_of, kept, recv, out, ld_even, ld_odd, p2k, p2s, p2r, p3k, p3s, p3r, ost,
    ld_sem, s2_sem, r2_sem, s3_sem, r3_sem, o_sem,
):
    yh, x, c, yl, z = place()
    peer_a = device(yh, x + 1 - 2 * (x % 2), c, yl, z)
    peer_b = device(yh, 3 - x, c, yl, z)
    peer_y = device(1 - yh, x, c, yl, z)
    greet((peer_a, peer_b, peer_y))

    ld = (ld_even, ld_odd)

    def loads(n, b):
        rows = pl.ds(pl.multiple_of(n * CROWS, CROWS), CROWS)
        return [
            pltpu.make_async_copy(source.at[:, h, rows, :], ld[b].at[h, pl.ds(g * UNITS, UNITS)], ld_sem.at[b, h, g])
            for h in range(2)
            for g, source in enumerate((kept, recv))
        ]

    def send_x(n, b, h):
        return pltpu.make_async_remote_copy(
            p2s.at[b, h], p2r.at[n, h], s2_sem.at[b, h], r2_sem.at[n, h],
            device_id=(peer_b, peer_a)[h], device_id_type=MESH,
        )

    def send_y(n, b):
        return pltpu.make_async_remote_copy(
            p3s.at[b], p3r.at[n], s3_sem.at[b], r3_sem.at[n], device_id=peer_y, device_id_type=MESH
        )

    def store(n, b, h):
        return pltpu.make_async_copy(
            ost.at[b, h], out.at[:, pl.ds(pl.multiple_of(h * 512 + n * CROWS, CROWS), CROWS), :], o_sem.at[b, h]
        )

    for load in loads(0, 0):
        load.start()

    def first(n, b):
        @pl.when(n + 1 < CHUNKS)
        def _():
            for load in loads(n + 1, 1 - b):
                load.start()

        for load in loads(n, b):
            load.wait()
        for h in range(2):
            @pl.when(n >= 2)
            def _():
                send_x(n - 2, b, h).wait_send()

            @pl.loop(0, LAYERS)
            def _(layer):
                total = None
                for q in range(4):
                    at = (h * LAYERS + layer) * 4 + q
                    term = ld[b][h, slot_of[at]].astype(jnp.float32) * weight_of[at]
                    total = term if total is None else total + term
                p2k[b, h, layer] = total[:, 0:256]
                p2s[b, h, layer] = total[:, 256:512].astype(jnp.bfloat16)

            send_x(n, b, h).start()

    def second(n, b):
        @pl.when(n >= 2)
        def _():
            send_y(n - 2, b).wait_send()

        for h in range(2):
            send_x(n, b, h).wait_recv()

            @pl.loop(0, LAYERS)
            def _(layer):
                total = p2k[b, h, layer] + p2r[n, h, layer].astype(jnp.float32)
                p3k[b, h, layer] = total[:, 0:128]
                p3s[b, h, layer] = total[:, 128:256].astype(jnp.bfloat16)

        send_y(n, b).start()

    def third(n, b):
        send_y(n, b).wait_recv()
        for h in range(2):
            @pl.when(n >= 2)
            def _():
                store(n - 2, b, h).wait()

            @pl.loop(0, LAYERS)
            def _(layer):
                ost[b, h, layer] = p3k[b, h, layer] + p3r[n, h, layer].astype(jnp.float32)

            store(n, b, h).start()

    @pl.loop(0, CHUNKS // 2 + 1)
    def _(it):
        for b in range(2):
            n = it * 2 + b

            @pl.when(n < CHUNKS)
            def _():
                first(n, b)

            @pl.when((n >= 1) & (n < CHUNKS + 1))
            def _():
                second(n - 1, 1 - b)

            @pl.when(n >= 2)
            def _():
                third(n - 2, b)

    for b in range(2):
        n = CHUNKS - 2 + b
        send_y(n, b).wait_send()
        for h in range(2):
            send_x(n, b, h).wait_send()
            store(n, b, h).wait()


def tables(section_code, boundaries):
    replica = (section_code >= 4).astype(jnp.int32) + (section_code >= 9).astype(jnp.int32)
    part = section_code - jnp.where(replica == 0, 0, jnp.where(replica == 1, 4, 9))
    low = boundaries[replica, part]
    high = boundaries[replica, part + 1]
    own = lax.axis_index("section")
    x = (own // 2) % 4
    base = own - 2 * x
    mate = own + 1 - 2 * (own % 2)
    slots, weights = [], []
    layers = jnp.arange(LAYERS, dtype=jnp.int32)
    for partner_x in (x + 1 - 2 * (x % 2), 3 - x):
        partner = base + 2 * partner_x
        partner_mate = partner + 1 - 2 * (partner % 2)
        for q, section in enumerate((own, mate, partner, partner_mate)):
            slot = layers - low[section]
            live = (slot >= 0) & (layers < high[section])
            slots.append(jnp.where(live, 2 * slot + (q % 2) + UNITS * (q // 2), 0))
            weights.append(live.astype(jnp.float32))
    order = lambda v: jnp.stack(v).reshape(2, 4, LAYERS).transpose(0, 2, 1).reshape(-1)
    return replica, order(slots).astype(jnp.int32), order(weights)


def per_device(activations, cotangents, section_code, boundaries, micro_counts):
    replica, slot_of, weight_of = tables(section_code, boundaries)
    row_limit = MBT * micro_counts[replica[lax.axis_index("section")]]
    live_rows = (jnp.arange(ROWS, dtype=jnp.int32) < row_limit)[None, :, None]
    masked = jnp.where(live_rows, cotangents[0], jnp.zeros((), jnp.bfloat16))
    any_spec = pl.BlockSpec(memory_space=pl.ANY)
    smem_spec = pl.BlockSpec(memory_space=pltpu.SMEM)
    dma = pltpu.SemaphoreType.DMA
    blocks = jax.ShapeDtypeStruct((UNITS, 2, 512, 512), jnp.bfloat16)
    kept, recv, _ = pl.pallas_call(
        gather_multiply,
        name="gather_multiply",
        out_shape=(blocks, blocks, jax.ShapeDtypeStruct((SLOTS, ROWS, WIDTH), jnp.bfloat16)),
        in_specs=[any_spec] * 2,
        out_specs=(any_spec,) * 3,
        scratch_shapes=[
            pltpu.VMEM((UNITS, ROWS, 1024), jnp.bfloat16),
            pltpu.VMEM((2, ROWS, WIDTH), jnp.bfloat16),
            pltpu.VMEM((2, 2, 512, 512), jnp.bfloat16),
            pltpu.VMEM((2, 2, 512, 512), jnp.bfloat16),
            dma((SLOTS,)), dma((SLOTS,)), dma((SLOTS,)), dma((SLOTS,)), dma((SLOTS,)),
            dma((8, UNITS)), dma((8, UNITS)), dma((2,)), dma((2,)), dma((2, 2)), dma((UNITS, 2)),
        ],
        compiler_params=pltpu.CompilerParams(
            collective_id=0, has_side_effects=True, vmem_limit_bytes=56 << 20
        ),
    )(masked, activations[0])
    return pl.pallas_call(
        merge,
        name="merge",
        out_shape=jax.ShapeDtypeStruct((LAYERS, WIDTH, 128), jnp.float32),
        in_specs=[smem_spec, smem_spec, any_spec, any_spec],
        out_specs=any_spec,
        scratch_shapes=[
            pltpu.VMEM((2, 2 * UNITS, CROWS, 512), jnp.bfloat16),
            pltpu.VMEM((2, 2 * UNITS, CROWS, 512), jnp.bfloat16),
            pltpu.VMEM((2, 2, LAYERS, CROWS, 256), jnp.float32),
            pltpu.VMEM((2, 2, LAYERS, CROWS, 256), jnp.bfloat16),
            pltpu.VMEM((CHUNKS, 2, LAYERS, CROWS, 256), jnp.bfloat16),
            pltpu.VMEM((2, 2, LAYERS, CROWS, 128), jnp.float32),
            pltpu.VMEM((2, 2, LAYERS, CROWS, 128), jnp.bfloat16),
            pltpu.VMEM((CHUNKS, 2, LAYERS, CROWS, 128), jnp.bfloat16),
            pltpu.VMEM((2, 2, LAYERS, CROWS, 128), jnp.float32),
            dma((2, 2, 2)), dma((2, 2)), dma((CHUNKS, 2)), dma((2,)), dma((CHUNKS,)), dma((2, 2)),
        ],
        compiler_params=pltpu.CompilerParams(
            collective_id=1, has_side_effects=True, vmem_limit_bytes=56 << 20
        ),
    )(slot_of, weight_of, kept, recv)


def solution(mesh):
    placed = (P("section", None, None, "tp"), P("section", None, None, "tp"), P(), P(), P())
    return jax.shard_map(
        per_device, mesh=mesh, in_specs=placed, out_specs=P(None, "tp", "section"), check_vma=False
    )
```

```python
import functools

import jax
import jax.numpy as jnp
from jax import lax
from jax.experimental import pallas as pl
from jax.experimental.pallas import tpu as pltpu
from jax.sharding import PartitionSpec as P

MBT = 256
MESH = pl.DeviceIdType.MESH
SLOTS = 5
UNITS = 2 * SLOTS
ROWS = 1024
WIDTH = 1024
LAYERS = 16
CHUNKS = 8
CROWS = 512 // CHUNKS


def place():
    section = lax.axis_index("section")
    tp = lax.axis_index("tp")
    return section // 8, (section // 2) % 4, section % 2, tp // 4, tp % 4


def device(yh, x, c, yl, z):
    return ((yh * 4 + x) * 2 + c, yl * 4 + z)


def greet(peers):
    barrier = pltpu.get_barrier_semaphore()
    for peer in peers:
        pl.semaphore_signal(barrier, inc=1, device_id=peer, device_id_type=MESH)
    pl.semaphore_wait(barrier, len(peers))


def gather_multiply(
    code, micro, c_ref, a_ref, kept, recv, a2, cbuf, abuf, stk, sts,
    loc_sem, cs_sem, cr_sem, as_sem, ar_sem, ms_sem, mr_sem, al_sem, k_sem, ps_sem, pr_sem,
):
    yh, x, c, yl, z = place()
    xa = x + 1 - 2 * (x % 2)
    xb = 3 - x
    mate = device(yh, x, 1 - c, yl, z)
    ypeer = device(yh, x, c, 1 - yl, z)
    zplus = device(yh, x, c, yl, (z + 1) % 4)
    zminus = device(yh, x, c, yl, (z + 3) % 4)
    peer_a = device(yh, xa, c, yl, z)
    peer_b = device(yh, xb, c, yl, z)
    greet((mate, ypeer, zplus, zminus, peer_a, peer_b))
    turn = 1 + 2 * (x % 2)

    def column(yy, zz):
        place_x = ((zz % 4 - x + 4) * turn) % 4
        place_y = (yy - yh + 2) % 2
        return pl.multiple_of((place_x * 2 + place_y) * 128, 128)

    def shard(s, yy, zz, row=0, rows=ROWS):
        return cbuf.at[s, pl.ds(row, rows), pl.ds(column(yy, zz), 128)]

    def own_c(j):
        return pltpu.make_async_copy(
            c_ref.at[j, :, pl.ds(pl.multiple_of(c * 128, 128), 128)], shard(2 * j, yl, z), loc_sem.at[j]
        )

    def mate_c(j):
        return pltpu.make_async_remote_copy(
            c_ref.at[j, :, pl.ds(pl.multiple_of((1 - c) * 128, 128), 128)],
            shard(2 * j + 1, yl, z), cs_sem.at[j], cr_sem.at[j], device_id=mate, device_id_type=MESH,
        )

    def mate_a(j):
        return pltpu.make_async_remote_copy(
            a_ref.at[j], a2.at[j], as_sem.at[j], ar_sem.at[j], device_id=mate, device_id_type=MESH
        )

    half = ROWS // 2
    own_section = (yh * 4 + x) * 2 + c
    limits = [
        MBT * micro[section_part(code, section)[0]] for section in (own_section, own_section + 1 - 2 * c)
    ]

    def message(kind, s):
        if kind <= 2:
            ref, target = shard(s, yl, z), (ypeer, zplus, zminus)[kind]
        elif kind <= 4:
            ref, target = shard(s, 1 - yl, z), (zplus, zminus)[kind - 3]
        elif kind == 5:
            ref, target = shard(s, yl, z + 3, 0, half), zplus
        elif kind == 6:
            ref, target = shard(s, yl, z + 1, half, half), zminus
        else:
            ref, target = shard(s, yl, z + 2), ypeer
        return pltpu.make_async_remote_copy(
            ref, ref, ms_sem.at[kind, s], mr_sem.at[kind, s], device_id=target, device_id_type=MESH
        )

    def load_own(j):
        return pltpu.make_async_copy(a_ref.at[j], abuf.at[0], al_sem.at[0])

    def load_mate(j):
        return pltpu.make_async_copy(a2.at[j], abuf.at[1], al_sem.at[1])

    def keep(s, b):
        return pltpu.make_async_copy(stk.at[b], kept.at[s], k_sem.at[b])

    def swap(s, b, h):
        return pltpu.make_async_remote_copy(
            sts.at[b, h], recv.at[s, h], ps_sem.at[b, h], pr_sem.at[s, h],
            device_id=(peer_a, peer_b)[h], device_id_type=MESH,
        )

    for j in range(SLOTS):
        own_c(j).start()
        mate_c(j).start()
    load_own(0).start()
    for j in range(SLOTS):
        mate_a(j).start()

    def compute(s, b):
        j = s // 2
        if b == 0:
            mate_a(j).wait_recv()
            load_mate(j).start()
            load_own(j).wait()
        else:
            @pl.when(j < SLOTS - 1)
            def _():
                load_own(j + 1).start()

            load_mate(j).wait()

        @pl.when(j > 0)
        def _():
            keep(s - 2, b).wait()
            swap(s - 2, b, 0).wait_send()
            swap(s - 2, b, 1).wait_send()

        for h in range(2):
            @pl.loop(0, 2)
            def _(tile):
                at = pl.multiple_of(tile * 256, 256)
                block = lax.dot_general(
                    abuf[b, :, pl.ds(h * 512 + at, 256)], cbuf[s],
                    (((0,), (0,)), ((), ())), preferred_element_type=jnp.float32,
                ).astype(jnp.bfloat16)
                rows = pl.ds(at, 256)
                if h == 0:
                    sts[b, 0, rows, :] = block[:, 256:768]
                    stk[b, 0, rows, 0:256] = block[:, 0:256]
                    stk[b, 0, rows, 256:512] = block[:, 768:1024]
                else:
                    sts[b, 1, rows, 0:256] = block[:, 768:1024]
                    sts[b, 1, rows, 256:512] = block[:, 512:768]
                    stk[b, 1, rows, :] = block[:, 0:512]

            swap(s, b, h).start()
        keep(s, b).start()

    @pl.loop(0, UNITS + 3)
    def _(it):
        @pl.when(it < UNITS)
        def _():
            @pl.when(it % 2 == 0)
            def _():
                own_c(it // 2).wait()

            @pl.when(it % 2 == 1)
            def _():
                mate_c(it // 2).wait_recv()

            own_column = pl.ds(column(yl, z), 128)
            limit = jnp.where(it % 2 == 0, limits[0], limits[1])
            live = (lax.broadcasted_iota(jnp.int32, (ROWS, 128), 0) < limit).astype(jnp.float32)
            cbuf[it, :, own_column] = (cbuf[it, :, own_column].astype(jnp.float32) * live).astype(jnp.bfloat16)
            for kind in (0, 1, 2):
                message(kind, it).start()

        @pl.when((it >= 1) & (it < UNITS + 1))
        def _():
            s = it - 1
            message(0, s).wait_recv()
            message(3, s).start()
            message(4, s).start()
            message(1, s).wait_recv()
            message(5, s).start()
            message(2, s).wait_recv()
            message(6, s).start()

        @pl.when((it >= 2) & (it < UNITS + 2))
        def _():
            s = it - 2
            message(5, s).wait_recv()
            message(6, s).wait_recv()
            message(7, s).start()

        @pl.when(it >= 3)
        def _():
            s = it - 3
            message(3, s).wait_recv()
            message(4, s).wait_recv()
            message(7, s).wait_recv()

            @pl.when(s % 2 == 0)
            def _():
                compute(s, 0)

            @pl.when(s % 2 == 1)
            def _():
                compute(s, 1)

    for b in range(2):
        s = UNITS - 2 + b
        keep(s, b).wait()
        swap(s, b, 0).wait_send()
        swap(s, b, 1).wait_send()
    for j in range(SLOTS):
        mate_c(j).wait_send()
        mate_a(j).wait_send()

    @pl.loop(0, UNITS)
    def _(s):
        for kind in range(8):
            message(kind, s).wait_send()
        for h in range(2):
            swap(s, 0, h).wait_recv()


def merge(
    code, bounds, kept, recv, own_sum, peer_sum, ld_even, ld_odd, p2k, p2s, p2r, p3k, p3s, slot_of, weight_of,
    ld_sem, s2_sem, r2_sem, s3_sem, r3_sem, o_sem,
):
    yh, x, c, yl, z = place()
    xa = x + 1 - 2 * (x % 2)
    xb = 3 - x
    peer_a = device(yh, xa, c, yl, z)
    peer_b = device(yh, xb, c, yl, z)
    peer_y = device(1 - yh, x, c, yl, z)
    ld = (ld_even, ld_odd)

    def loads(n, b):
        rows = pl.ds(pl.multiple_of(n * CROWS, CROWS), CROWS)
        return [
            pltpu.make_async_copy(source.at[:, h, rows, :], ld[b].at[h, pl.ds(g * UNITS, UNITS)], ld_sem.at[b, h, g])
            for h in range(2)
            for g, source in enumerate((kept, recv))
        ]

    def send_x(n, b, h):
        return pltpu.make_async_remote_copy(
            p2s.at[b, h], p2r.at[n, h], s2_sem.at[b, h], r2_sem.at[n, h],
            device_id=(peer_b, peer_a)[h], device_id_type=MESH,
        )

    def send_y(n, b, h):
        rows = pl.ds(pl.multiple_of(h * 512 + n * CROWS, CROWS), CROWS)
        return pltpu.make_async_remote_copy(
            p3s.at[b, h], peer_sum.at[:, rows, :], s3_sem.at[b, h], r3_sem.at[n, h],
            device_id=peer_y, device_id_type=MESH,
        )

    def store(n, b, h):
        return pltpu.make_async_copy(
            p3k.at[b, h], own_sum.at[:, pl.ds(pl.multiple_of(h * 512 + n * CROWS, CROWS), CROWS), :], o_sem.at[b, h]
        )

    for load in loads(0, 0):
        load.start()
    for h, partner in enumerate((xa, xb)):
        sections = ((x, c), (x, 1 - c), (partner, c), (partner, 1 - c))
        for q, (sx, sc) in enumerate(sections):
            replica, part = section_part(code, (yh * 4 + sx) * 2 + sc)
            low = bounds[replica, part]
            high = bounds[replica, part + 1]

            @pl.loop(0, LAYERS)
            def _(layer):
                live = (layer >= low) & (layer < high)
                at = (h * LAYERS + layer) * 4 + q
                slot_of[at] = jnp.where(live, 2 * (layer - low) + (q % 2) + UNITS * (q // 2), 0)
                weight_of[at] = jnp.where(live, 1.0, 0.0)

    greet((peer_a, peer_b, peer_y))

    def first(n, b):
        @pl.when(n + 1 < CHUNKS)
        def _():
            for load in loads(n + 1, 1 - b):
                load.start()

        for load in loads(n, b):
            load.wait()
        for h in range(2):
            @pl.when(n >= 2)
            def _():
                send_x(n - 2, b, h).wait_send()

            @pl.loop(0, LAYERS)
            def _(layer):
                total = None
                for q in range(4):
                    at = (h * LAYERS + layer) * 4 + q
                    term = ld[b][h, slot_of[at]].astype(jnp.float32) * weight_of[at]
                    total = term if total is None else total + term
                p2k[b, h, layer] = total[:, 0:256]
                p2s[b, h, layer] = total[:, 256:512].astype(jnp.bfloat16)

            send_x(n, b, h).start()

    def second(n, b):
        @pl.when(n >= 2)
        def _():
            for h in range(2):
                send_y(n - 2, b, h).wait_send()
                store(n - 2, b, h).wait()

        for h in range(2):
            send_x(n, b, h).wait_recv()

            @pl.loop(0, LAYERS)
            def _(layer):
                total = p2k[b, h, layer] + p2r[n, h, layer].astype(jnp.float32)
                p3k[b, h, layer] = total[:, 0:128]
                p3s[b, h, layer] = total[:, 128:256].astype(jnp.bfloat16)

            send_y(n, b, h).start()
            store(n, b, h).start()

    @pl.loop(0, CHUNKS // 2 + 1)
    def _(it):
        for b in range(2):
            n = it * 2 + b

            @pl.when(n < CHUNKS)
            def _():
                first(n, b)

            @pl.when((n >= 1) & (n < CHUNKS + 1))
            def _():
                second(n - 1, 1 - b)

    for b in range(2):
        n = CHUNKS - 2 + b
        for h in range(2):
            send_x(n, b, h).wait_send()
            send_y(n, b, h).wait_send()
            store(n, b, h).wait()

    @pl.loop(0, CHUNKS)
    def _(n):
        for h in range(2):
            send_y(n, 0, h).wait_recv()


def section_part(code, section):
    value = code[section]
    second = jnp.where(value >= 4, 1, 0)
    third = jnp.where(value >= 9, 1, 0)
    return second + third, value - 4 * second - 5 * third


def per_device(activations, cotangents, section_code, boundaries, micro_counts):
    any_spec = pl.BlockSpec(memory_space=pl.ANY)
    smem_spec = pl.BlockSpec(memory_space=pltpu.SMEM)
    dma = pltpu.SemaphoreType.DMA
    blocks = jax.ShapeDtypeStruct((UNITS, 2, 512, 512), jnp.bfloat16)
    kept, recv, _ = pl.pallas_call(
        gather_multiply,
        name="gather_multiply",
        out_shape=(blocks, blocks, jax.ShapeDtypeStruct((SLOTS, ROWS, WIDTH), jnp.bfloat16)),
        in_specs=[smem_spec] * 2 + [any_spec] * 2,
        out_specs=(any_spec,) * 3,
        scratch_shapes=[
            pltpu.VMEM((UNITS, ROWS, 1024), jnp.bfloat16),
            pltpu.VMEM((2, ROWS, WIDTH), jnp.bfloat16),
            pltpu.VMEM((2, 2, 512, 512), jnp.bfloat16),
            pltpu.VMEM((2, 2, 512, 512), jnp.bfloat16),
            dma((SLOTS,)), dma((SLOTS,)), dma((SLOTS,)), dma((SLOTS,)), dma((SLOTS,)),
            dma((8, UNITS)), dma((8, UNITS)), dma((2,)), dma((2,)), dma((2, 2)), dma((UNITS, 2)),
        ],
        compiler_params=pltpu.CompilerParams(
            collective_id=0, has_side_effects=True, vmem_limit_bytes=56 << 20
        ),
    )(section_code, micro_counts, cotangents[0], activations[0])
    own_sum, peer_sum = pl.pallas_call(
        merge,
        name="merge",
        out_shape=(
            jax.ShapeDtypeStruct((LAYERS, WIDTH, 128), jnp.float32),
            jax.ShapeDtypeStruct((LAYERS, WIDTH, 128), jnp.bfloat16),
        ),
        in_specs=[smem_spec, smem_spec, any_spec, any_spec],
        out_specs=(any_spec, any_spec),
        scratch_shapes=[
            pltpu.VMEM((2, 2 * UNITS, CROWS, 512), jnp.bfloat16),
            pltpu.VMEM((2, 2 * UNITS, CROWS, 512), jnp.bfloat16),
            pltpu.VMEM((2, 2, LAYERS, CROWS, 256), jnp.float32),
            pltpu.VMEM((2, 2, LAYERS, CROWS, 256), jnp.bfloat16),
            pltpu.VMEM((CHUNKS, 2, LAYERS, CROWS, 256), jnp.bfloat16),
            pltpu.VMEM((2, 2, LAYERS, CROWS, 128), jnp.float32),
            pltpu.VMEM((2, 2, LAYERS, CROWS, 128), jnp.bfloat16),
            pltpu.SMEM((2 * LAYERS * 4,), jnp.int32),
            pltpu.SMEM((2 * LAYERS * 4,), jnp.float32),
            dma((2, 2, 2)), dma((2, 2)), dma((CHUNKS, 2)), dma((2, 2)), dma((CHUNKS, 2)), dma((2, 2)),
        ],
        compiler_params=pltpu.CompilerParams(
            collective_id=1, has_side_effects=True, vmem_limit_bytes=56 << 20
        ),
    )(section_code, boundaries, kept, recv)
    return own_sum + peer_sum.astype(jnp.float32)


def solution(mesh):
    placed = (P("section", None, None, "tp"), P("section", None, None, "tp"), P(), P(), P())
    return jax.shard_map(
        per_device, mesh=mesh, in_specs=placed, out_specs=P(None, "tp", "section"), check_vma=False
    )
```

```python
import functools

import jax
import jax.numpy as jnp
from jax import lax
from jax.experimental import pallas as pl
from jax.experimental.pallas import tpu as pltpu
from jax.sharding import PartitionSpec as P

MBT = 256
MESH = pl.DeviceIdType.MESH
SLOTS = 5
UNITS = 2 * SLOTS
ROWS = 1024
WIDTH = 1024
LAYERS = 16
CHUNKS = 16
SPLIT = 176
CROWS = 512 // CHUNKS


def place():
    section = lax.axis_index("section")
    tp = lax.axis_index("tp")
    return section // 8, (section // 2) % 4, section % 2, tp // 4, tp % 4


def device(yh, x, c, yl, z):
    return ((yh * 4 + x) * 2 + c, yl * 4 + z)


def greet(peers):
    barrier = pltpu.get_barrier_semaphore()
    for peer in peers:
        pl.semaphore_signal(barrier, inc=1, device_id=peer, device_id_type=MESH)
    pl.semaphore_wait(barrier, len(peers))


def gradients(
    code, bounds, micro, c_ref, a_ref, own_sum, peer_sum, kept, recv, a2,
    cbuf, abuf, stk, sts, ld_even, ld_odd, p2k, p2s, p2r, p3k, p3s, slot_of, weight_of,
    loc_sem, cs_sem, cr_sem, as_sem, ar_sem, ms_sem, mr_sem, al_sem, k_sem, ps_sem, pr_sem,
    ld_sem, s2_sem, r2_sem, s3_sem, r3_sem, o_sem,
):
    yh, x, c, yl, z = place()
    xa = x + 1 - 2 * (x % 2)
    xb = 3 - x
    mate = device(yh, x, 1 - c, yl, z)
    ypeer = device(yh, x, c, 1 - yl, z)
    zplus = device(yh, x, c, yl, (z + 1) % 4)
    zminus = device(yh, x, c, yl, (z + 3) % 4)
    peer_a = device(yh, xa, c, yl, z)
    peer_b = device(yh, xb, c, yl, z)
    peer_y = device(1 - yh, x, c, yl, z)
    ld = (ld_even, ld_odd)
    greet((mate, ypeer, zplus, zminus, peer_a, peer_b, peer_y))
    turn = 1 + 2 * (x % 2)

    def column(yy, zz):
        place_x = ((zz % 4 - x + 4) * turn) % 4
        place_y = (yy - yh + 2) % 2
        return pl.multiple_of((place_x * 2 + place_y) * 128, 128)

    def shard(s, yy, zz, row=0, rows=ROWS):
        return cbuf.at[s, pl.ds(row, rows), pl.ds(column(yy, zz), 128)]

    def own_c(j):
        return pltpu.make_async_copy(
            c_ref.at[j, :, pl.ds(pl.multiple_of(c * 128, 128), 128)], shard(2 * j, yl, z), loc_sem.at[j]
        )

    def mate_c(j):
        return pltpu.make_async_remote_copy(
            c_ref.at[j, :, pl.ds(pl.multiple_of((1 - c) * 128, 128), 128)],
            shard(2 * j + 1, yl, z), cs_sem.at[j], cr_sem.at[j], device_id=mate, device_id_type=MESH,
        )

    def mate_a(j):
        return pltpu.make_async_remote_copy(
            a_ref.at[j], a2.at[j], as_sem.at[j], ar_sem.at[j], device_id=mate, device_id_type=MESH
        )

    half = ROWS // 2
    own_section = (yh * 4 + x) * 2 + c
    limits = [
        MBT * micro[section_part(code, section)[0]] for section in (own_section, own_section + 1 - 2 * c)
    ]

    def message(kind, s):
        if kind <= 2:
            ref, target = shard(s, yl, z), (ypeer, zplus, zminus)[kind]
        elif kind <= 4:
            ref, target = shard(s, 1 - yl, z, SPLIT, ROWS - SPLIT), (zplus, zminus)[kind - 3]
        elif kind == 5:
            ref, target = shard(s, yl, z + 3, 0, half), zplus
        elif kind == 6:
            ref, target = shard(s, yl, z + 1, half, half), zminus
        elif kind == 7:
            ref, target = shard(s, yl, z + 2), ypeer
        else:
            ref, target = shard(s, yl, (z + 3, z + 1)[kind - 8], 0, SPLIT), ypeer
        return pltpu.make_async_remote_copy(
            ref, ref, ms_sem.at[kind, s], mr_sem.at[kind, s], device_id=target, device_id_type=MESH
        )

    def load_own(j):
        return pltpu.make_async_copy(a_ref.at[j], abuf.at[0], al_sem.at[0])

    def load_mate(j):
        return pltpu.make_async_copy(a2.at[j], abuf.at[1], al_sem.at[1])

    def keep(s, b):
        return pltpu.make_async_copy(stk.at[b], kept.at[s], k_sem.at[b])

    def swap(s, b, h, tile):
        rows = pl.ds(pl.multiple_of(tile * 256, 256), 256)
        return pltpu.make_async_remote_copy(
            sts.at[b, h, rows], recv.at[s, h, rows], ps_sem.at[b, h, tile], pr_sem.at[s, h, tile],
            device_id=(peer_a, peer_b)[h], device_id_type=MESH,
        )

    for j in range(SLOTS):
        own_c(j).start()
        mate_c(j).start()
    load_own(0).start()
    for j in range(SLOTS):
        mate_a(j).start()

    def compute(s, b):
        j = s // 2
        if b == 0:
            mate_a(j).wait_recv()
            load_mate(j).start()
            load_own(j).wait()
        else:
            @pl.when(j < SLOTS - 1)
            def _():
                load_own(j + 1).start()

            load_mate(j).wait()

        @pl.when(j > 0)
        def _():
            keep(s - 2, b).wait()
            for h in range(2):
                for tile in range(2):
                    swap(s - 2, b, h, tile).wait_send()

        @pl.loop(0, 2)
        def _(tile):
            at = pl.multiple_of(tile * 256, 256)
            rows = pl.ds(at, 256)
            for h in range(2):
                block = lax.dot_general(
                    abuf[b, :, pl.ds(h * 512 + at, 256)], cbuf[s],
                    (((0,), (0,)), ((), ())), preferred_element_type=jnp.float32,
                ).astype(jnp.bfloat16)
                if h == 0:
                    sts[b, 0, rows, :] = block[:, 256:768]
                    stk[b, 0, rows, 0:256] = block[:, 0:256]
                    stk[b, 0, rows, 256:512] = block[:, 768:1024]
                else:
                    sts[b, 1, rows, 0:256] = block[:, 768:1024]
                    sts[b, 1, rows, 256:512] = block[:, 512:768]
                    stk[b, 1, rows, :] = block[:, 0:512]
                swap(s, b, h, tile).start()

        keep(s, b).start()

    @pl.loop(0, UNITS + 3)
    def _(it):
        @pl.when(it < UNITS)
        def _():
            @pl.when(it % 2 == 0)
            def _():
                own_c(it // 2).wait()

            @pl.when(it % 2 == 1)
            def _():
                mate_c(it // 2).wait_recv()

            own_column = pl.ds(column(yl, z), 128)
            limit = jnp.where(it % 2 == 0, limits[0], limits[1])
            live = (lax.broadcasted_iota(jnp.int32, (ROWS, 128), 0) < limit).astype(jnp.float32)
            cbuf[it, :, own_column] = (cbuf[it, :, own_column].astype(jnp.float32) * live).astype(jnp.bfloat16)
            for kind in (0, 1, 2):
                message(kind, it).start()

        @pl.when((it >= 1) & (it < UNITS + 1))
        def _():
            s = it - 1
            message(0, s).wait_recv()
            message(3, s).start()
            message(4, s).start()
            message(1, s).wait_recv()
            message(5, s).start()
            message(8, s).start()
            message(2, s).wait_recv()
            message(6, s).start()
            message(9, s).start()

        @pl.when((it >= 2) & (it < UNITS + 2))
        def _():
            s = it - 2
            message(5, s).wait_recv()
            message(6, s).wait_recv()
            message(7, s).start()

        @pl.when(it >= 3)
        def _():
            s = it - 3
            message(3, s).wait_recv()
            message(4, s).wait_recv()
            for kind in (7, 8, 9):
                message(kind, s).wait_recv()

            @pl.when(s % 2 == 0)
            def _():
                compute(s, 0)

            @pl.when(s % 2 == 1)
            def _():
                compute(s, 1)

    for h, partner in enumerate((xa, xb)):
        sections = ((x, c), (x, 1 - c), (partner, c), (partner, 1 - c))
        for q, (sx, sc) in enumerate(sections):
            replica, part = section_part(code, (yh * 4 + sx) * 2 + sc)
            low = bounds[replica, part]
            high = bounds[replica, part + 1]

            @pl.loop(0, LAYERS)
            def _(layer):
                live = (layer >= low) & (layer < high)
                at = (h * LAYERS + layer) * 4 + q
                slot_of[at] = jnp.where(live, 2 * (layer - low) + (q % 2) + UNITS * (q // 2), 0)
                weight_of[at] = jnp.where(live, 1.0, 0.0)

    for b in range(2):
        keep(UNITS - 2 + b, b).wait()

    def arrived(tile):
        @pl.loop(0, UNITS)
        def _(s):
            for h in range(2):
                swap(s, 0, h, tile).wait_recv()

    def loads(n, b):
        rows = pl.ds(pl.multiple_of(n * CROWS, CROWS), CROWS)
        return [
            pltpu.make_async_copy(source.at[:, h, rows, :], ld[b].at[h, pl.ds(g * UNITS, UNITS)], ld_sem.at[b, h, g])
            for h in range(2)
            for g, source in enumerate((kept, recv))
        ]

    def send_x(n, b, h):
        return pltpu.make_async_remote_copy(
            p2s.at[b, h], p2r.at[n, h], s2_sem.at[b, h], r2_sem.at[n, h],
            device_id=(peer_b, peer_a)[h], device_id_type=MESH,
        )

    def send_y(n, b, h):
        rows = pl.ds(pl.multiple_of(h * 512 + n * CROWS, CROWS), CROWS)
        return pltpu.make_async_remote_copy(
            p3s.at[b, h], peer_sum.at[:, rows, :], s3_sem.at[b, h], r3_sem.at[n, h],
            device_id=peer_y, device_id_type=MESH,
        )

    def store(n, b, h):
        return pltpu.make_async_copy(
            p3k.at[b, h], own_sum.at[:, pl.ds(pl.multiple_of(h * 512 + n * CROWS, CROWS), CROWS), :], o_sem.at[b, h]
        )

    def first(n, b):
        if b == 0:
            @pl.when(n == 0)
            def _():
                arrived(0)
                for load in loads(0, 0):
                    load.start()

        else:
            @pl.when(n == CHUNKS // 2 - 1)
            def _():
                arrived(1)

        @pl.when(n + 1 < CHUNKS)
        def _():
            for load in loads(n + 1, 1 - b):
                load.start()

        for load in loads(n, b):
            load.wait()
        for h in range(2):
            @pl.when(n >= 2)
            def _():
                send_x(n - 2, b, h).wait_send()

            @pl.loop(0, LAYERS)
            def _(layer):
                total = None
                for q in range(4):
                    at = (h * LAYERS + layer) * 4 + q
                    term = ld[b][h, slot_of[at]].astype(jnp.float32) * weight_of[at]
                    total = term if total is None else total + term
                p2k[b, h, layer] = total[:, 0:256]
                p2s[b, h, layer] = total[:, 256:512].astype(jnp.bfloat16)

            send_x(n, b, h).start()

    def second(n, b):
        @pl.when(n >= 2)
        def _():
            for h in range(2):
                send_y(n - 2, b, h).wait_send()
                store(n - 2, b, h).wait()

        for h in range(2):
            send_x(n, b, h).wait_recv()

            @pl.loop(0, LAYERS)
            def _(layer):
                total = p2k[b, h, layer] + p2r[n, h, layer].astype(jnp.float32)
                p3k[b, h, layer] = total[:, 0:128]
                p3s[b, h, layer] = total[:, 128:256].astype(jnp.bfloat16)

            send_y(n, b, h).start()
            store(n, b, h).start()

    @pl.loop(0, CHUNKS // 2 + 1)
    def _(it):
        for b in range(2):
            n = it * 2 + b

            @pl.when(n < CHUNKS)
            def _():
                first(n, b)

            @pl.when((n >= 1) & (n < CHUNKS + 1))
            def _():
                second(n - 1, 1 - b)

    for b in range(2):
        n = CHUNKS - 2 + b
        for h in range(2):
            send_x(n, b, h).wait_send()
            send_y(n, b, h).wait_send()
            store(n, b, h).wait()

    for b in range(2):
        for h in range(2):
            for tile in range(2):
                swap(UNITS - 2 + b, b, h, tile).wait_send()
    for j in range(SLOTS):
        mate_c(j).wait_send()
        mate_a(j).wait_send()

    @pl.loop(0, UNITS)
    def _(s):
        for kind in range(10):
            message(kind, s).wait_send()

    @pl.loop(0, CHUNKS)
    def _(n):
        for h in range(2):
            send_y(n, 0, h).wait_recv()


def section_part(code, section):
    value = code[section]
    second = jnp.where(value >= 4, 1, 0)
    third = jnp.where(value >= 9, 1, 0)
    return second + third, value - 4 * second - 5 * third


def per_device(activations, cotangents, section_code, boundaries, micro_counts):
    any_spec = pl.BlockSpec(memory_space=pl.ANY)
    smem_spec = pl.BlockSpec(memory_space=pltpu.SMEM)
    dma = pltpu.SemaphoreType.DMA
    blocks = jax.ShapeDtypeStruct((UNITS, 2, 512, 512), jnp.bfloat16)
    own_sum, peer_sum, _, _, _ = pl.pallas_call(
        gradients,
        name="gradients",
        out_shape=(
            jax.ShapeDtypeStruct((LAYERS, WIDTH, 128), jnp.float32),
            jax.ShapeDtypeStruct((LAYERS, WIDTH, 128), jnp.bfloat16),
            blocks,
            blocks,
            jax.ShapeDtypeStruct((SLOTS, ROWS, WIDTH), jnp.bfloat16),
        ),
        in_specs=[smem_spec] * 3 + [any_spec] * 2,
        out_specs=(any_spec,) * 5,
        scratch_shapes=[
            pltpu.VMEM((UNITS, ROWS, 1024), jnp.bfloat16),
            pltpu.VMEM((2, ROWS, WIDTH), jnp.bfloat16),
            pltpu.VMEM((2, 2, 512, 512), jnp.bfloat16),
            pltpu.VMEM((2, 2, 512, 512), jnp.bfloat16),
            pltpu.VMEM((2, 2 * UNITS, CROWS, 512), jnp.bfloat16),
            pltpu.VMEM((2, 2 * UNITS, CROWS, 512), jnp.bfloat16),
            pltpu.VMEM((2, 2, LAYERS, CROWS, 256), jnp.float32),
            pltpu.VMEM((2, 2, LAYERS, CROWS, 256), jnp.bfloat16),
            pltpu.VMEM((CHUNKS, 2, LAYERS, CROWS, 256), jnp.bfloat16),
            pltpu.VMEM((2, 2, LAYERS, CROWS, 128), jnp.float32),
            pltpu.VMEM((2, 2, LAYERS, CROWS, 128), jnp.bfloat16),
            pltpu.SMEM((2 * LAYERS * 4,), jnp.int32),
            pltpu.SMEM((2 * LAYERS * 4,), jnp.float32),
            dma((SLOTS,)), dma((SLOTS,)), dma((SLOTS,)), dma((SLOTS,)), dma((SLOTS,)),
            dma((10, UNITS)), dma((10, UNITS)), dma((2,)), dma((2,)), dma((2, 2, 2)), dma((UNITS, 2, 2)),
            dma((2, 2, 2)), dma((2, 2)), dma((CHUNKS, 2)), dma((2, 2)), dma((CHUNKS, 2)), dma((2, 2)),
        ],
        compiler_params=pltpu.CompilerParams(
            collective_id=0, has_side_effects=True, vmem_limit_bytes=60 << 20
        ),
    )(section_code, boundaries, micro_counts, cotangents[0], activations[0])
    return own_sum + peer_sum.astype(jnp.float32)


def solution(mesh):
    placed = (P("section", None, None, "tp"), P("section", None, None, "tp"), P(), P(), P())
    return jax.shard_map(
        per_device, mesh=mesh, in_specs=placed, out_specs=P(None, "tp", "section"), check_vma=False
    )
```

```python
import functools

import jax
import jax.numpy as jnp
from jax import lax
from jax.experimental import pallas as pl
from jax.experimental.pallas import tpu as pltpu
from jax.sharding import PartitionSpec as P

MBT = 256
MESH = pl.DeviceIdType.MESH
SLOTS = 5
UNITS = 2 * SLOTS
ROWS = 1024
WIDTH = 1024
LAYERS = 16
CHUNKS = 16
SPLIT = 176
EARLY = 3
LATE = LAYERS - EARLY
EROWS = 64
CROWS = 512 // CHUNKS


def place():
    section = lax.axis_index("section")
    tp = lax.axis_index("tp")
    return section // 8, (section // 2) % 4, section % 2, tp // 4, tp % 4


def device(yh, x, c, yl, z):
    return ((yh * 4 + x) * 2 + c, yl * 4 + z)


def greet(peers):
    barrier = pltpu.get_barrier_semaphore()
    for peer in peers:
        pl.semaphore_signal(barrier, inc=1, device_id=peer, device_id_type=MESH)
    pl.semaphore_wait(barrier, len(peers))


def gradients(
    code, bounds, micro, c_ref, a_ref, own_sum, peer_sum, kept, recv, a2,
    cbuf, abuf, stk, sts, ld_even, ld_odd, p2k, p2s, p2r, p3k, p3s, slot_of, weight_of,
    le_even, le_odd, q2k, q2s, q2r, q3k, q3s,
    loc_sem, cs_sem, cr_sem, as_sem, ar_sem, ms_sem, mr_sem, al_sem, k_sem, ps_sem, pr_sem,
    ld_sem, s2_sem, r2_sem, s3_sem, r3_sem, o_sem,
    le_sem, t2_sem, u2_sem, t3_sem, u3_sem, v_sem,
):
    yh, x, c, yl, z = place()
    xa = x + 1 - 2 * (x % 2)
    xb = 3 - x
    mate = device(yh, x, 1 - c, yl, z)
    ypeer = device(yh, x, c, 1 - yl, z)
    zplus = device(yh, x, c, yl, (z + 1) % 4)
    zminus = device(yh, x, c, yl, (z + 3) % 4)
    peer_a = device(yh, xa, c, yl, z)
    peer_b = device(yh, xb, c, yl, z)
    peer_y = device(1 - yh, x, c, yl, z)
    ld = (ld_even, ld_odd)
    le = (le_even, le_odd)
    greet((mate, ypeer, zplus, zminus, peer_a, peer_b, peer_y))
    turn = 1 + 2 * (x % 2)

    def column(yy, zz):
        place_x = ((zz % 4 - x + 4) * turn) % 4
        place_y = (yy - yh + 2) % 2
        return pl.multiple_of((place_x * 2 + place_y) * 128, 128)

    def shard(s, yy, zz, row=0, rows=ROWS):
        return cbuf.at[s, pl.ds(row, rows), pl.ds(column(yy, zz), 128)]

    def own_c(j):
        return pltpu.make_async_copy(
            c_ref.at[j, :, pl.ds(pl.multiple_of(c * 128, 128), 128)], shard(2 * j, yl, z), loc_sem.at[j]
        )

    def mate_c(j):
        return pltpu.make_async_remote_copy(
            c_ref.at[j, :, pl.ds(pl.multiple_of((1 - c) * 128, 128), 128)],
            shard(2 * j + 1, yl, z), cs_sem.at[j], cr_sem.at[j], device_id=mate, device_id_type=MESH,
        )

    def mate_a(j):
        return pltpu.make_async_remote_copy(
            a_ref.at[j], a2.at[j], as_sem.at[j], ar_sem.at[j], device_id=mate, device_id_type=MESH
        )

    half = ROWS // 2
    own_section = (yh * 4 + x) * 2 + c
    limits = [
        MBT * micro[section_part(code, section)[0]] for section in (own_section, own_section + 1 - 2 * c)
    ]

    def message(kind, s):
        if kind <= 2:
            ref, target = shard(s, yl, z), (ypeer, zplus, zminus)[kind]
        elif kind <= 4:
            ref, target = shard(s, 1 - yl, z, SPLIT, ROWS - SPLIT), (zplus, zminus)[kind - 3]
        elif kind == 5:
            ref, target = shard(s, yl, z + 3, 0, half), zplus
        elif kind == 6:
            ref, target = shard(s, yl, z + 1, half, half), zminus
        elif kind == 7:
            ref, target = shard(s, yl, z + 2), ypeer
        else:
            ref, target = shard(s, yl, (z + 3, z + 1)[kind - 8], 0, SPLIT), ypeer
        return pltpu.make_async_remote_copy(
            ref, ref, ms_sem.at[kind, s], mr_sem.at[kind, s], device_id=target, device_id_type=MESH
        )

    def load_own(j):
        return pltpu.make_async_copy(a_ref.at[j], abuf.at[0], al_sem.at[0])

    def load_mate(j):
        return pltpu.make_async_copy(a2.at[j], abuf.at[1], al_sem.at[1])

    def keep(s, b):
        return pltpu.make_async_copy(stk.at[b], kept.at[s], k_sem.at[b])

    def swap(s, b, h, tile):
        rows = pl.ds(pl.multiple_of(tile * 256, 256), 256)
        return pltpu.make_async_remote_copy(
            sts.at[b, h, rows], recv.at[s, h, rows], ps_sem.at[b, h, tile], pr_sem.at[s, h, tile],
            device_id=(peer_a, peer_b)[h], device_id_type=MESH,
        )

    for j in range(SLOTS):
        own_c(j).start()
        mate_c(j).start()
    load_own(0).start()
    for j in range(SLOTS):
        mate_a(j).start()

    def compute(s, b):
        j = s // 2
        if b == 0:
            mate_a(j).wait_recv()
            load_mate(j).start()
            load_own(j).wait()
        else:
            @pl.when(j < SLOTS - 1)
            def _():
                load_own(j + 1).start()

            load_mate(j).wait()

        @pl.when(j > 0)
        def _():
            keep(s - 2, b).wait()
            for h in range(2):
                for tile in range(2):
                    swap(s - 2, b, h, tile).wait_send()

        @pl.loop(0, 2)
        def _(tile):
            at = pl.multiple_of(tile * 256, 256)
            rows = pl.ds(at, 256)
            for h in range(2):
                block = lax.dot_general(
                    abuf[b, :, pl.ds(h * 512 + at, 256)], cbuf[s],
                    (((0,), (0,)), ((), ())), preferred_element_type=jnp.float32,
                ).astype(jnp.bfloat16)
                if h == 0:
                    sts[b, 0, rows, :] = block[:, 256:768]
                    stk[b, 0, rows, 0:256] = block[:, 0:256]
                    stk[b, 0, rows, 256:512] = block[:, 768:1024]
                else:
                    sts[b, 1, rows, 0:256] = block[:, 768:1024]
                    sts[b, 1, rows, 256:512] = block[:, 512:768]
                    stk[b, 1, rows, :] = block[:, 0:512]
                swap(s, b, h, tile).start()

        keep(s, b).start()

    def tables():
        for h, partner in enumerate((xa, xb)):
            sections = ((x, c), (x, 1 - c), (partner, c), (partner, 1 - c))
            for q, (sx, sc) in enumerate(sections):
                replica, part = section_part(code, (yh * 4 + sx) * 2 + sc)
                low = bounds[replica, part]
                high = bounds[replica, part + 1]

                @pl.loop(0, LAYERS)
                def _(layer):
                    live = (layer >= low) & (layer < high)
                    at = (h * LAYERS + layer) * 4 + q
                    slot_of[at] = jnp.where(live, 2 * (layer - low) + (q % 2), 0) + UNITS * (q // 2)
                    weight_of[at] = jnp.where(live, 1.0, 0.0)

    def early_loads(layer, block, b):
        count = 2 * layer + 2
        rows = pl.ds(pl.multiple_of(block * EROWS, EROWS), EROWS)
        return [
            pltpu.make_async_copy(
                source.at[pl.ds(0, count), h, rows, :], le[b].at[h, pl.ds(g * count, count)], le_sem.at[b, h, g]
            )
            for h in range(2)
            for g, source in enumerate((kept, recv))
        ]

    def early_x(layer, h):
        b = layer % 2
        return pltpu.make_async_remote_copy(
            q2s.at[b, h], q2r.at[layer, h], t2_sem.at[b, h], u2_sem.at[layer, h],
            device_id=(peer_b, peer_a)[h], device_id_type=MESH,
        )

    def early_y(layer, h):
        b = layer % 2
        return pltpu.make_async_remote_copy(
            q3s.at[b, h], peer_sum.at[layer, pl.ds(h * 512, 512), :], t3_sem.at[b, h], u3_sem.at[layer, h],
            device_id=peer_y, device_id_type=MESH,
        )

    def early_store(layer, h):
        b = layer % 2
        return pltpu.make_async_copy(q3k.at[b, h], own_sum.at[layer, pl.ds(h * 512, 512), :], v_sem.at[b, h])

    def early_first(layer):
        p = layer % 2
        count = 2 * layer + 2
        for s in (2 * layer, 2 * layer + 1):
            for h in range(2):
                for tile in range(2):
                    swap(s, 0, h, tile).wait_recv()
        if layer >= 2:
            for h in range(2):
                early_x(layer - 2, h).wait_send()
        for load in early_loads(layer, 0, 0):
            load.start()

        @pl.loop(0, 512 // EROWS // 2)
        def _(pair):
            for b in range(2):
                block = pair * 2 + b

                @pl.when(block + 1 < 512 // EROWS)
                def _():
                    for load in early_loads(layer, block + 1, 1 - b):
                        load.start()

                for load in early_loads(layer, block, b):
                    load.wait()
                rows = pl.ds(pl.multiple_of(block * EROWS, EROWS), EROWS)
                for h in range(2):
                    total = None
                    for q in range(4):
                        at = (h * LAYERS + layer) * 4 + q
                        slot = slot_of[at] + (q // 2) * (count - UNITS)
                        term = le[b][h, slot].astype(jnp.float32) * weight_of[at]
                        total = term if total is None else total + term
                    q2k[p, h, rows, :] = total[:, 0:256]
                    q2s[p, h, rows, :] = total[:, 256:512].astype(jnp.bfloat16)

        for h in range(2):
            early_x(layer, h).start()

    def early_second(layer):
        p = layer % 2
        for h in range(2):
            if layer >= 2:
                early_y(layer - 2, h).wait_send()
                early_store(layer - 2, h).wait()
            early_x(layer, h).wait_recv()

            @pl.loop(0, 512 // EROWS)
            def _(block):
                rows = pl.ds(pl.multiple_of(block * EROWS, EROWS), EROWS)
                total = q2k[p, h, rows, :] + q2r[layer, h, rows, :].astype(jnp.float32)
                q3k[p, h, rows, :] = total[:, 0:128]
                q3s[p, h, rows, :] = total[:, 128:256].astype(jnp.bfloat16)

            early_y(layer, h).start()
            early_store(layer, h).start()

    @pl.loop(0, UNITS + 1)
    def _(it):
        @pl.when(it < UNITS)
        def _():
            @pl.when(it % 2 == 0)
            def _():
                own_c(it // 2).wait()

            @pl.when(it % 2 == 1)
            def _():
                mate_c(it // 2).wait_recv()

            own_column = pl.ds(column(yl, z), 128)
            limit = jnp.where(it % 2 == 0, limits[0], limits[1])
            live = (lax.broadcasted_iota(jnp.int32, (ROWS, 128), 0) < limit).astype(jnp.float32)
            cbuf[it, :, own_column] = (cbuf[it, :, own_column].astype(jnp.float32) * live).astype(jnp.bfloat16)
            for kind in (0, 1, 2):
                message(kind, it).start()

        @pl.when(it >= 1)
        def _():
            message(5, it - 1).wait_recv()
            message(6, it - 1).wait_recv()
            message(7, it - 1).start()

        pl.when(it == 1)(tables)
        for layer in range(EARLY):
            pl.when(it == 2 * layer + 5)(functools.partial(early_first, layer))
            if layer < EARLY - 1:
                pl.when(it == 2 * layer + 7)(functools.partial(early_second, layer))

        @pl.when(it < UNITS)
        def _():
            message(0, it).wait_recv()
            message(3, it).start()
            message(4, it).start()
            message(1, it).wait_recv()
            message(5, it).start()
            message(8, it).start()
            message(2, it).wait_recv()
            message(6, it).start()
            message(9, it).start()

        @pl.when(it >= 1)
        def _():
            s = it - 1
            for kind in (3, 4, 7, 8, 9):
                message(kind, s).wait_recv()

            @pl.when(s % 2 == 0)
            def _():
                compute(s, 0)

            @pl.when(s % 2 == 1)
            def _():
                compute(s, 1)

    for b in range(2):
        keep(UNITS - 2 + b, b).wait()

    def arrived(tile):
        for s in range(2 * EARLY, UNITS):
            for h in range(2):
                swap(s, 0, h, tile).wait_recv()

    def loads(n, b):
        rows = pl.ds(pl.multiple_of(n * CROWS, CROWS), CROWS)
        return [
            pltpu.make_async_copy(source.at[:, h, rows, :], ld[b].at[h, pl.ds(g * UNITS, UNITS)], ld_sem.at[b, h, g])
            for h in range(2)
            for g, source in enumerate((kept, recv))
        ]

    def send_x(n, b, h):
        return pltpu.make_async_remote_copy(
            p2s.at[b, h], p2r.at[n, h], s2_sem.at[b, h], r2_sem.at[n, h],
            device_id=(peer_b, peer_a)[h], device_id_type=MESH,
        )

    def send_y(n, b, h):
        rows = pl.ds(pl.multiple_of(h * 512 + n * CROWS, CROWS), CROWS)
        return pltpu.make_async_remote_copy(
            p3s.at[b, h], peer_sum.at[pl.ds(EARLY, LATE), rows, :], s3_sem.at[b, h], r3_sem.at[n, h],
            device_id=peer_y, device_id_type=MESH,
        )

    def store(n, b, h):
        return pltpu.make_async_copy(
            p3k.at[b, h], own_sum.at[pl.ds(EARLY, LATE), pl.ds(pl.multiple_of(h * 512 + n * CROWS, CROWS), CROWS), :], o_sem.at[b, h]
        )

    def first(n, b):
        if b == 0:
            @pl.when(n == 0)
            def _():
                arrived(0)
                for load in loads(0, 0):
                    load.start()

        else:
            @pl.when(n == CHUNKS // 2 - 1)
            def _():
                arrived(1)

        @pl.when(n + 1 < CHUNKS)
        def _():
            for load in loads(n + 1, 1 - b):
                load.start()

        for load in loads(n, b):
            load.wait()
        for h in range(2):
            @pl.when(n >= 2)
            def _():
                send_x(n - 2, b, h).wait_send()

            @pl.loop(0, LATE)
            def _(layer):
                total = None
                for q in range(4):
                    at = (h * LAYERS + EARLY + layer) * 4 + q
                    term = ld[b][h, slot_of[at]].astype(jnp.float32) * weight_of[at]
                    total = term if total is None else total + term
                p2k[b, h, layer] = total[:, 0:256]
                p2s[b, h, layer] = total[:, 256:512].astype(jnp.bfloat16)

            send_x(n, b, h).start()

    def second(n, b):
        @pl.when(n >= 2)
        def _():
            for h in range(2):
                send_y(n - 2, b, h).wait_send()
                store(n - 2, b, h).wait()

        for h in range(2):
            send_x(n, b, h).wait_recv()

            @pl.loop(0, LATE)
            def _(layer):
                total = p2k[b, h, layer] + p2r[n, h, layer].astype(jnp.float32)
                p3k[b, h, layer] = total[:, 0:128]
                p3s[b, h, layer] = total[:, 128:256].astype(jnp.bfloat16)

            send_y(n, b, h).start()
            store(n, b, h).start()

    @pl.loop(0, CHUNKS // 2 + 1)
    def _(it):
        @pl.when(it == 1)
        def _():
            early_second(EARLY - 1)

        for b in range(2):
            n = it * 2 + b

            @pl.when(n < CHUNKS)
            def _():
                first(n, b)

            @pl.when((n >= 1) & (n < CHUNKS + 1))
            def _():
                second(n - 1, 1 - b)

    for b in range(2):
        n = CHUNKS - 2 + b
        for h in range(2):
            send_x(n, b, h).wait_send()
            send_y(n, b, h).wait_send()
            store(n, b, h).wait()

    for b in range(2):
        for h in range(2):
            for tile in range(2):
                swap(UNITS - 2 + b, b, h, tile).wait_send()
    for j in range(SLOTS):
        mate_c(j).wait_send()
        mate_a(j).wait_send()

    for layer in range(EARLY):
        for h in range(2):
            early_y(layer, h).wait_recv()
            if layer >= EARLY - 2:
                early_x(layer, h).wait_send()
                early_y(layer, h).wait_send()
                early_store(layer, h).wait()

    @pl.loop(0, UNITS)
    def _(s):
        for kind in range(10):
            message(kind, s).wait_send()

    @pl.loop(0, CHUNKS)
    def _(n):
        for h in range(2):
            send_y(n, 0, h).wait_recv()


def section_part(code, section):
    value = code[section]
    second = jnp.where(value >= 4, 1, 0)
    third = jnp.where(value >= 9, 1, 0)
    return second + third, value - 4 * second - 5 * third


def per_device(activations, cotangents, section_code, boundaries, micro_counts):
    any_spec = pl.BlockSpec(memory_space=pl.ANY)
    smem_spec = pl.BlockSpec(memory_space=pltpu.SMEM)
    dma = pltpu.SemaphoreType.DMA
    blocks = jax.ShapeDtypeStruct((UNITS, 2, 512, 512), jnp.bfloat16)
    own_sum, peer_sum, _, _, _ = pl.pallas_call(
        gradients,
        name="gradients",
        out_shape=(
            jax.ShapeDtypeStruct((LAYERS, WIDTH, 128), jnp.float32),
            jax.ShapeDtypeStruct((LAYERS, WIDTH, 128), jnp.bfloat16),
            blocks,
            blocks,
            jax.ShapeDtypeStruct((SLOTS, ROWS, WIDTH), jnp.bfloat16),
        ),
        in_specs=[smem_spec] * 3 + [any_spec] * 2,
        out_specs=(any_spec,) * 5,
        scratch_shapes=[
            pltpu.VMEM((UNITS, ROWS, 1024), jnp.bfloat16),
            pltpu.VMEM((2, ROWS, WIDTH), jnp.bfloat16),
            pltpu.VMEM((2, 2, 512, 512), jnp.bfloat16),
            pltpu.VMEM((2, 2, 512, 512), jnp.bfloat16),
            pltpu.VMEM((2, 2 * UNITS, CROWS, 512), jnp.bfloat16),
            pltpu.VMEM((2, 2 * UNITS, CROWS, 512), jnp.bfloat16),
            pltpu.VMEM((2, 2, LATE, CROWS, 256), jnp.float32),
            pltpu.VMEM((2, 2, LATE, CROWS, 256), jnp.bfloat16),
            pltpu.VMEM((CHUNKS, 2, LATE, CROWS, 256), jnp.bfloat16),
            pltpu.VMEM((2, 2, LATE, CROWS, 128), jnp.float32),
            pltpu.VMEM((2, 2, LATE, CROWS, 128), jnp.bfloat16),
            pltpu.SMEM((2 * LAYERS * 4,), jnp.int32),
            pltpu.SMEM((2 * LAYERS * 4,), jnp.float32),
            pltpu.VMEM((2, 4 * EARLY, EROWS, 512), jnp.bfloat16),
            pltpu.VMEM((2, 4 * EARLY, EROWS, 512), jnp.bfloat16),
            pltpu.VMEM((2, 2, 512, 256), jnp.float32),
            pltpu.VMEM((2, 2, 512, 256), jnp.bfloat16),
            pltpu.VMEM((EARLY, 2, 512, 256), jnp.bfloat16),
            pltpu.VMEM((2, 2, 512, 128), jnp.float32),
            pltpu.VMEM((2, 2, 512, 128), jnp.bfloat16),
            dma((SLOTS,)), dma((SLOTS,)), dma((SLOTS,)), dma((SLOTS,)), dma((SLOTS,)),
            dma((10, UNITS)), dma((10, UNITS)), dma((2,)), dma((2,)), dma((2, 2, 2)), dma((UNITS, 2, 2)),
            dma((2, 2, 2)), dma((2, 2)), dma((CHUNKS, 2)), dma((2, 2)), dma((CHUNKS, 2)), dma((2, 2)),
            dma((2, 2, 2)), dma((2, 2)), dma((EARLY, 2)), dma((2, 2)), dma((EARLY, 2)), dma((2, 2)),
        ],
        compiler_params=pltpu.CompilerParams(
            collective_id=0, has_side_effects=True, vmem_limit_bytes=60 << 20
        ),
    )(section_code, boundaries, micro_counts, cotangents[0], activations[0])
    return own_sum + peer_sum.astype(jnp.float32)


def solution(mesh):
    placed = (P("section", None, None, "tp"), P("section", None, None, "tp"), P(), P(), P())
    return jax.shard_map(
        per_device, mesh=mesh, in_specs=placed, out_specs=P(None, "tp", "section"), check_vma=False
    )
```

```python
import functools

import jax
import jax.numpy as jnp
from jax import lax
from jax.experimental import pallas as pl
from jax.experimental.pallas import tpu as pltpu
from jax.sharding import PartitionSpec as P

MBT = 256
MESH = pl.DeviceIdType.MESH
SLOTS = 5
UNITS = 2 * SLOTS
ROWS = 1024
WIDTH = 1024
LAYERS = 16
CHUNKS = 32
BUFFERS = 4
DELAY = 3
SPLIT = 176
EARLY = 3
LATE = LAYERS - EARLY
EROWS = 64
CROWS = 512 // CHUNKS


def place():
    section = lax.axis_index("section")
    tp = lax.axis_index("tp")
    return section // 8, (section // 2) % 4, section % 2, tp // 4, tp % 4


def device(yh, x, c, yl, z):
    return ((yh * 4 + x) * 2 + c, yl * 4 + z)


def greet(peers):
    barrier = pltpu.get_barrier_semaphore()
    for peer in peers:
        pl.semaphore_signal(barrier, inc=1, device_id=peer, device_id_type=MESH)
    pl.semaphore_wait(barrier, len(peers))


def gradients(
    code, bounds, micro, c_ref, a_ref, own_sum, peer_sum, kept, recv, a2,
    cbuf, abuf, stk, sts, ld_even, ld_odd, p2k, p2s, p2r, p3k, p3s, slot_of, weight_of,
    le_even, le_odd, q2k, q2s, q2r, q3k, q3s,
    loc_sem, cs_sem, cr_sem, as_sem, ar_sem, ms_sem, mr_sem, al_sem, k_sem, ps_sem, pr_sem,
    ld_sem, s2_sem, r2_sem, s3_sem, r3_sem, o_sem,
    le_sem, t2_sem, u2_sem, t3_sem, u3_sem, v_sem,
):
    yh, x, c, yl, z = place()
    xa = x + 1 - 2 * (x % 2)
    xb = 3 - x
    mate = device(yh, x, 1 - c, yl, z)
    ypeer = device(yh, x, c, 1 - yl, z)
    zplus = device(yh, x, c, yl, (z + 1) % 4)
    zminus = device(yh, x, c, yl, (z + 3) % 4)
    peer_a = device(yh, xa, c, yl, z)
    peer_b = device(yh, xb, c, yl, z)
    peer_y = device(1 - yh, x, c, yl, z)
    ld = (ld_even, ld_odd)
    le = (le_even, le_odd)
    turn = 1 + 2 * (x % 2)

    def column(yy, zz):
        place_x = ((zz % 4 - x + 4) * turn) % 4
        place_y = (yy - yh + 2) % 2
        return pl.multiple_of((place_x * 2 + place_y) * 128, 128)

    def shard(s, yy, zz, row=0, rows=ROWS):
        return cbuf.at[s, pl.ds(row, rows), pl.ds(column(yy, zz), 128)]

    def own_c(j):
        return pltpu.make_async_copy(
            c_ref.at[j, :, pl.ds(pl.multiple_of(c * 128, 128), 128)], shard(2 * j, yl, z), loc_sem.at[j]
        )

    def mate_c(j):
        return pltpu.make_async_remote_copy(
            c_ref.at[j, :, pl.ds(pl.multiple_of((1 - c) * 128, 128), 128)],
            shard(2 * j + 1, yl, z), cs_sem.at[j], cr_sem.at[j], device_id=mate, device_id_type=MESH,
        )

    def mate_a(j):
        return pltpu.make_async_remote_copy(
            a_ref.at[j], a2.at[j], as_sem.at[j], ar_sem.at[j], device_id=mate, device_id_type=MESH
        )

    half = ROWS // 2
    own_section = (yh * 4 + x) * 2 + c
    limits = [
        MBT * micro[section_part(code, section)[0]] for section in (own_section, own_section + 1 - 2 * c)
    ]

    def message(kind, s):
        if kind <= 2:
            ref, target = shard(s, yl, z), (ypeer, zplus, zminus)[kind]
        elif kind <= 4:
            ref, target = shard(s, 1 - yl, z, SPLIT, ROWS - SPLIT), (zplus, zminus)[kind - 3]
        elif kind == 5:
            ref, target = shard(s, yl, z + 3, 0, half), zplus
        elif kind == 6:
            ref, target = shard(s, yl, z + 1, half, half), zminus
        elif kind == 7:
            ref, target = shard(s, yl, z + 2), ypeer
        else:
            ref, target = shard(s, yl, (z + 3, z + 1)[kind - 8], 0, SPLIT), ypeer
        return pltpu.make_async_remote_copy(
            ref, ref, ms_sem.at[kind, s], mr_sem.at[kind, s], device_id=target, device_id_type=MESH
        )

    def load_own(j):
        return pltpu.make_async_copy(a_ref.at[j], abuf.at[0], al_sem.at[0])

    def load_mate(j):
        return pltpu.make_async_copy(a2.at[j], abuf.at[1], al_sem.at[1])

    def keep(s, b):
        return pltpu.make_async_copy(stk.at[b], kept.at[s], k_sem.at[b])

    def swap(s, b, h, tile):
        rows = pl.ds(pl.multiple_of(tile * 256, 256), 256)
        return pltpu.make_async_remote_copy(
            sts.at[b, h, rows], recv.at[s, h, rows], ps_sem.at[b, h, tile], pr_sem.at[s, h, tile],
            device_id=(peer_a, peer_b)[h], device_id_type=MESH,
        )

    def mask_own(s):
        own_column = pl.ds(column(yl, z), 128)
        limit = jnp.where(s % 2 == 0, limits[0], limits[1])
        live = (lax.broadcasted_iota(jnp.int32, (ROWS, 128), 0) < limit).astype(jnp.float32)
        cbuf[s, :, own_column] = (cbuf[s, :, own_column].astype(jnp.float32) * live).astype(jnp.bfloat16)

    own_c(0).start()
    load_own(0).start()
    own_c(0).wait()
    mask_own(0)
    greet((mate, ypeer, zplus, zminus, peer_a, peer_b, peer_y))
    for kind in (0, 1, 2):
        message(kind, 0).start()
    for j in range(SLOTS):
        if j > 0:
            own_c(j).start()
        mate_c(j).start()
    for j in range(SLOTS):
        mate_a(j).start()

    def compute(s, b):
        j = s // 2
        if b == 0:
            mate_a(j).wait_recv()
            load_mate(j).start()
            load_own(j).wait()
        else:
            @pl.when(j < SLOTS - 1)
            def _():
                load_own(j + 1).start()

            load_mate(j).wait()

        @pl.when(j > 0)
        def _():
            keep(s - 2, b).wait()
            for h in range(2):
                for tile in range(2):
                    swap(s - 2, b, h, tile).wait_send()

        @pl.loop(0, 2)
        def _(tile):
            at = pl.multiple_of(tile * 256, 256)
            rows = pl.ds(at, 256)
            for h in range(2):
                block = lax.dot_general(
                    abuf[b, :, pl.ds(h * 512 + at, 256)], cbuf[s],
                    (((0,), (0,)), ((), ())), preferred_element_type=jnp.float32,
                ).astype(jnp.bfloat16)
                if h == 0:
                    sts[b, 0, rows, :] = block[:, 256:768]
                    stk[b, 0, rows, 0:256] = block[:, 0:256]
                    stk[b, 0, rows, 256:512] = block[:, 768:1024]
                else:
                    sts[b, 1, rows, 0:256] = block[:, 768:1024]
                    sts[b, 1, rows, 256:512] = block[:, 512:768]
                    stk[b, 1, rows, :] = block[:, 0:512]
                swap(s, b, h, tile).start()

        keep(s, b).start()

    def tables():
        for h, partner in enumerate((xa, xb)):
            sections = ((x, c), (x, 1 - c), (partner, c), (partner, 1 - c))
            for q, (sx, sc) in enumerate(sections):
                replica, part = section_part(code, (yh * 4 + sx) * 2 + sc)
                low = bounds[replica, part]
                high = bounds[replica, part + 1]

                @pl.loop(0, LAYERS)
                def _(layer):
                    live = (layer >= low) & (layer < high)
                    at = (h * LAYERS + layer) * 4 + q
                    slot_of[at] = jnp.where(live, 2 * (layer - low) + (q % 2), 0) + UNITS * (q // 2)
                    weight_of[at] = jnp.where(live, 1.0, 0.0)

    def early_loads(layer, block, b):
        count = 2 * layer + 2
        rows = pl.ds(pl.multiple_of(block * EROWS, EROWS), EROWS)
        return [
            pltpu.make_async_copy(
                source.at[pl.ds(0, count), h, rows, :], le[b].at[h, pl.ds(g * count, count)], le_sem.at[b, h, g]
            )
            for h in range(2)
            for g, source in enumerate((kept, recv))
        ]

    def early_x(layer, h):
        b = layer % 2
        return pltpu.make_async_remote_copy(
            q2s.at[b, h], q2r.at[layer, h], t2_sem.at[b, h], u2_sem.at[layer, h],
            device_id=(peer_b, peer_a)[h], device_id_type=MESH,
        )

    def early_y(layer, h):
        b = layer % 2
        return pltpu.make_async_remote_copy(
            q3s.at[b, h], peer_sum.at[layer, pl.ds(h * 512, 512), :], t3_sem.at[b, h], u3_sem.at[layer, h],
            device_id=peer_y, device_id_type=MESH,
        )

    def early_store(layer, h):
        b = layer % 2
        return pltpu.make_async_copy(q3k.at[b, h], own_sum.at[layer, pl.ds(h * 512, 512), :], v_sem.at[b, h])

    def early_first(layer):
        p = layer % 2
        count = 2 * layer + 2
        for s in (2 * layer, 2 * layer + 1):
            for h in range(2):
                for tile in range(2):
                    swap(s, 0, h, tile).wait_recv()
        if layer >= 2:
            for h in range(2):
                early_x(layer - 2, h).wait_send()
        for load in early_loads(layer, 0, 0):
            load.start()

        @pl.loop(0, 512 // EROWS // 2)
        def _(pair):
            for b in range(2):
                block = pair * 2 + b

                @pl.when(block + 1 < 512 // EROWS)
                def _():
                    for load in early_loads(layer, block + 1, 1 - b):
                        load.start()

                for load in early_loads(layer, block, b):
                    load.wait()
                rows = pl.ds(pl.multiple_of(block * EROWS, EROWS), EROWS)
                for h in range(2):
                    total = None
                    for q in range(4):
                        at = (h * LAYERS + layer) * 4 + q
                        slot = slot_of[at] + (q // 2) * (count - UNITS)
                        term = le[b][h, slot].astype(jnp.float32) * weight_of[at]
                        total = term if total is None else total + term
                    q2k[p, h, rows, :] = total[:, 0:256]
                    q2s[p, h, rows, :] = total[:, 256:512].astype(jnp.bfloat16)

        for h in range(2):
            early_x(layer, h).start()

    def early_second(layer):
        p = layer % 2
        for h in range(2):
            if layer >= 2:
                early_y(layer - 2, h).wait_send()
                early_store(layer - 2, h).wait()
            early_x(layer, h).wait_recv()

            @pl.loop(0, 512 // EROWS)
            def _(block):
                rows = pl.ds(pl.multiple_of(block * EROWS, EROWS), EROWS)
                total = q2k[p, h, rows, :] + q2r[layer, h, rows, :].astype(jnp.float32)
                q3k[p, h, rows, :] = total[:, 0:128]
                q3s[p, h, rows, :] = total[:, 128:256].astype(jnp.bfloat16)

            early_y(layer, h).start()
            early_store(layer, h).start()

    @pl.loop(0, UNITS + 1)
    def _(it):
        @pl.when((it >= 1) & (it < UNITS))
        def _():
            @pl.when(it % 2 == 0)
            def _():
                own_c(it // 2).wait()

            @pl.when(it % 2 == 1)
            def _():
                mate_c(it // 2).wait_recv()

            mask_own(it)
            for kind in (0, 1, 2):
                message(kind, it).start()

        @pl.when(it >= 1)
        def _():
            message(5, it - 1).wait_recv()
            message(6, it - 1).wait_recv()
            message(7, it - 1).start()

        pl.when(it == 1)(tables)
        for layer in range(EARLY):
            pl.when(it == 2 * layer + 5)(functools.partial(early_first, layer))
            if layer < EARLY - 1:
                pl.when(it == 2 * layer + 7)(functools.partial(early_second, layer))

        @pl.when(it < UNITS)
        def _():
            message(0, it).wait_recv()
            message(3, it).start()
            message(4, it).start()
            message(1, it).wait_recv()
            message(5, it).start()
            message(8, it).start()
            message(2, it).wait_recv()
            message(6, it).start()
            message(9, it).start()

        @pl.when(it >= 1)
        def _():
            s = it - 1
            for kind in (3, 4, 7, 8, 9):
                message(kind, s).wait_recv()

            @pl.when(s % 2 == 0)
            def _():
                compute(s, 0)

            @pl.when(s % 2 == 1)
            def _():
                compute(s, 1)

    for b in range(2):
        keep(UNITS - 2 + b, b).wait()

    def arrived(tile):
        for s in range(2 * EARLY, UNITS):
            for h in range(2):
                swap(s, 0, h, tile).wait_recv()

    def loads(n, b):
        rows = pl.ds(pl.multiple_of(n * CROWS, CROWS), CROWS)
        return [
            pltpu.make_async_copy(source.at[:, h, rows, :], ld[b].at[h, pl.ds(g * UNITS, UNITS)], ld_sem.at[b, h, g])
            for h in range(2)
            for g, source in enumerate((kept, recv))
        ]

    def send_x(n, b, h):
        return pltpu.make_async_remote_copy(
            p2s.at[b, h], p2r.at[n, h], s2_sem.at[b, h], r2_sem.at[n, h],
            device_id=(peer_b, peer_a)[h], device_id_type=MESH,
        )

    def send_y(n, b, h):
        rows = pl.ds(pl.multiple_of(h * 512 + n * CROWS, CROWS), CROWS)
        return pltpu.make_async_remote_copy(
            p3s.at[b, h], peer_sum.at[pl.ds(EARLY, LATE), rows, :], s3_sem.at[b, h], r3_sem.at[n, h],
            device_id=peer_y, device_id_type=MESH,
        )

    def store(n, b, h):
        return pltpu.make_async_copy(
            p3k.at[b, h], own_sum.at[pl.ds(EARLY, LATE), pl.ds(pl.multiple_of(h * 512 + n * CROWS, CROWS), CROWS), :], o_sem.at[b, h]
        )

    def first(n, b):
        if b == 0:
            @pl.when(n == 0)
            def _():
                arrived(0)
                for load in loads(0, 0):
                    load.start()

        if b == (CHUNKS // 2 - 1) % BUFFERS:
            @pl.when(n == CHUNKS // 2 - 1)
            def _():
                arrived(1)

        @pl.when(n + 1 < CHUNKS)
        def _():
            for load in loads(n + 1, 1 - b % 2):
                load.start()

        for load in loads(n, b % 2):
            load.wait()
        for h in range(2):
            @pl.when(n >= BUFFERS)
            def _():
                send_x(n - BUFFERS, b, h).wait_send()

            @pl.loop(0, LATE)
            def _(layer):
                total = None
                for q in range(4):
                    at = (h * LAYERS + EARLY + layer) * 4 + q
                    term = ld[b % 2][h, slot_of[at]].astype(jnp.float32) * weight_of[at]
                    total = term if total is None else total + term
                p2k[b, h, layer] = total[:, 0:256]
                p2s[b, h, layer] = total[:, 256:512].astype(jnp.bfloat16)

            send_x(n, b, h).start()

    def second(n, b):
        d = b % 2

        @pl.when(n >= 2)
        def _():
            for h in range(2):
                send_y(n - 2, d, h).wait_send()
                store(n - 2, d, h).wait()

        for h in range(2):
            send_x(n, b, h).wait_recv()

            @pl.loop(0, LATE)
            def _(layer):
                total = p2k[b, h, layer] + p2r[n, h, layer].astype(jnp.float32)
                p3k[d, h, layer] = total[:, 0:128]
                p3s[d, h, layer] = total[:, 128:256].astype(jnp.bfloat16)

            send_y(n, d, h).start()
            store(n, d, h).start()

    @pl.loop(0, CHUNKS // BUFFERS + 1)
    def _(it):
        for b in range(BUFFERS):
            n = it * BUFFERS + b

            @pl.when(n < CHUNKS)
            def _():
                first(n, b)

            if b == 1:
                pl.when(it == 0)(functools.partial(early_second, EARLY - 1))

            @pl.when((n >= DELAY) & (n < CHUNKS + DELAY))
            def _():
                second(n - DELAY, (b - DELAY) % BUFFERS)

    for b in range(BUFFERS):
        for h in range(2):
            send_x(CHUNKS - BUFFERS + b, b, h).wait_send()
    for b in range(2):
        for h in range(2):
            send_y(CHUNKS - 2 + b, b, h).wait_send()
            store(CHUNKS - 2 + b, b, h).wait()

    for b in range(2):
        for h in range(2):
            for tile in range(2):
                swap(UNITS - 2 + b, b, h, tile).wait_send()
    for j in range(SLOTS):
        mate_c(j).wait_send()
        mate_a(j).wait_send()

    for layer in range(EARLY):
        for h in range(2):
            early_y(layer, h).wait_recv()
            if layer >= EARLY - 2:
                early_x(layer, h).wait_send()
                early_y(layer, h).wait_send()
                early_store(layer, h).wait()

    @pl.loop(0, UNITS)
    def _(s):
        for kind in range(10):
            message(kind, s).wait_send()

    @pl.loop(0, CHUNKS)
    def _(n):
        for h in range(2):
            send_y(n, 0, h).wait_recv()


def section_part(code, section):
    value = code[section]
    second = jnp.where(value >= 4, 1, 0)
    third = jnp.where(value >= 9, 1, 0)
    return second + third, value - 4 * second - 5 * third


def per_device(activations, cotangents, section_code, boundaries, micro_counts):
    any_spec = pl.BlockSpec(memory_space=pl.ANY)
    smem_spec = pl.BlockSpec(memory_space=pltpu.SMEM)
    dma = pltpu.SemaphoreType.DMA
    blocks = jax.ShapeDtypeStruct((UNITS, 2, 512, 512), jnp.bfloat16)
    own_sum, peer_sum, _, _, _ = pl.pallas_call(
        gradients,
        name="gradients",
        out_shape=(
            jax.ShapeDtypeStruct((LAYERS, WIDTH, 128), jnp.float32),
            jax.ShapeDtypeStruct((LAYERS, WIDTH, 128), jnp.bfloat16),
            blocks,
            blocks,
            jax.ShapeDtypeStruct((SLOTS, ROWS, WIDTH), jnp.bfloat16),
        ),
        in_specs=[smem_spec] * 3 + [any_spec] * 2,
        out_specs=(any_spec,) * 5,
        scratch_shapes=[
            pltpu.VMEM((UNITS, ROWS, 1024), jnp.bfloat16),
            pltpu.VMEM((2, ROWS, WIDTH), jnp.bfloat16),
            pltpu.VMEM((2, 2, 512, 512), jnp.bfloat16),
            pltpu.VMEM((2, 2, 512, 512), jnp.bfloat16),
            pltpu.VMEM((2, 2 * UNITS, CROWS, 512), jnp.bfloat16),
            pltpu.VMEM((2, 2 * UNITS, CROWS, 512), jnp.bfloat16),
            pltpu.VMEM((BUFFERS, 2, LATE, CROWS, 256), jnp.float32),
            pltpu.VMEM((BUFFERS, 2, LATE, CROWS, 256), jnp.bfloat16),
            pltpu.VMEM((CHUNKS, 2, LATE, CROWS, 256), jnp.bfloat16),
            pltpu.VMEM((2, 2, LATE, CROWS, 128), jnp.float32),
            pltpu.VMEM((2, 2, LATE, CROWS, 128), jnp.bfloat16),
            pltpu.SMEM((2 * LAYERS * 4,), jnp.int32),
            pltpu.SMEM((2 * LAYERS * 4,), jnp.float32),
            pltpu.VMEM((2, 4 * EARLY, EROWS, 512), jnp.bfloat16),
            pltpu.VMEM((2, 4 * EARLY, EROWS, 512), jnp.bfloat16),
            pltpu.VMEM((2, 2, 512, 256), jnp.float32),
            pltpu.VMEM((2, 2, 512, 256), jnp.bfloat16),
            pltpu.VMEM((EARLY, 2, 512, 256), jnp.bfloat16),
            pltpu.VMEM((2, 2, 512, 128), jnp.float32),
            pltpu.VMEM((2, 2, 512, 128), jnp.bfloat16),
            dma((SLOTS,)), dma((SLOTS,)), dma((SLOTS,)), dma((SLOTS,)), dma((SLOTS,)),
            dma((10, UNITS)), dma((10, UNITS)), dma((2,)), dma((2,)), dma((2, 2, 2)), dma((UNITS, 2, 2)),
            dma((2, 2, 2)), dma((BUFFERS, 2)), dma((CHUNKS, 2)), dma((2, 2)), dma((CHUNKS, 2)), dma((2, 2)),
            dma((2, 2, 2)), dma((2, 2)), dma((EARLY, 2)), dma((2, 2)), dma((EARLY, 2)), dma((2, 2)),
        ],
        compiler_params=pltpu.CompilerParams(
            collective_id=0, has_side_effects=True, vmem_limit_bytes=60 << 20
        ),
    )(section_code, boundaries, micro_counts, cotangents[0], activations[0])
    return own_sum + peer_sum.astype(jnp.float32)


def solution(mesh):
    placed = (P("section", None, None, "tp"), P("section", None, None, "tp"), P(), P(), P())
    return jax.shard_map(
        per_device, mesh=mesh, in_specs=placed, out_specs=P(None, "tp", "section"), check_vma=False
    )
```

```python
import functools

import jax
import jax.numpy as jnp
from jax import lax
from jax.experimental import pallas as pl
from jax.experimental.pallas import tpu as pltpu
from jax.sharding import PartitionSpec as P

MBT = 256
MESH = pl.DeviceIdType.MESH
SLOTS = 5
UNITS = 2 * SLOTS
ROWS = 1024
WIDTH = 1024
LAYERS = 16
CHUNKS = 32
BUFFERS = 4
DELAY = 3
SPLIT = 176
EARLY = 3
LATE = LAYERS - EARLY
EROWS = 64
CROWS = 512 // CHUNKS


def place():
    section = lax.axis_index("section")
    tp = lax.axis_index("tp")
    return section // 8, (section // 2) % 4, section % 2, tp // 4, tp % 4


def device(yh, x, c, yl, z):
    return ((yh * 4 + x) * 2 + c, yl * 4 + z)


def greet(peers):
    barrier = pltpu.get_barrier_semaphore()
    for peer in peers:
        pl.semaphore_signal(barrier, inc=1, device_id=peer, device_id_type=MESH)
    pl.semaphore_wait(barrier, len(peers))


def gradients(
    code, bounds, micro, c_ref, a_ref, own_sum, peer_sum, kept, recv, a2,
    cbuf, abuf, stk, sts, ld_even, ld_odd, p2k, p2s, p2r, p3k, p3s, slot_of, weight_of,
    le_even, le_odd, q2k, q2s, q2r, q3k, q3s,
    loc_sem, cs_sem, cr_sem, as_sem, ar_sem, ms_sem, mr_sem, al_sem, k_sem, ps_sem, pr_sem,
    ld_sem, s2_sem, r2_sem, s3_sem, r3_sem, o_sem,
    le_sem, t2_sem, u2_sem, t3_sem, u3_sem, v_sem,
):
    yh, x, c, yl, z = place()
    xa = x + 1 - 2 * (x % 2)
    xb = 3 - x
    mate = device(yh, x, 1 - c, yl, z)
    ypeer = device(yh, x, c, 1 - yl, z)
    zplus = device(yh, x, c, yl, (z + 1) % 4)
    zminus = device(yh, x, c, yl, (z + 3) % 4)
    peer_a = device(yh, xa, c, yl, z)
    peer_b = device(yh, xb, c, yl, z)
    peer_y = device(1 - yh, x, c, yl, z)
    ld = (ld_even, ld_odd)
    le = (le_even, le_odd)
    turn = 1 + 2 * (x % 2)

    def column(yy, zz):
        place_x = ((zz % 4 - x + 4) * turn) % 4
        place_y = (yy - yh + 2) % 2
        return pl.multiple_of((place_x * 2 + place_y) * 128, 128)

    def shard(s, yy, zz, row=0, rows=ROWS):
        return cbuf.at[s, pl.ds(row, rows), pl.ds(column(yy, zz), 128)]

    def own_c(j):
        return pltpu.make_async_copy(
            c_ref.at[j, :, pl.ds(pl.multiple_of(c * 128, 128), 128)], shard(2 * j, yl, z), loc_sem.at[j]
        )

    def mate_c(j):
        return pltpu.make_async_remote_copy(
            c_ref.at[j, :, pl.ds(pl.multiple_of((1 - c) * 128, 128), 128)],
            shard(2 * j + 1, yl, z), cs_sem.at[j], cr_sem.at[j], device_id=mate, device_id_type=MESH,
        )

    def mate_a(j):
        return pltpu.make_async_remote_copy(
            a_ref.at[j], a2.at[j], as_sem.at[j], ar_sem.at[j], device_id=mate, device_id_type=MESH
        )

    half = ROWS // 2
    own_section = (yh * 4 + x) * 2 + c
    limits = [
        MBT * micro[section_part(code, section)[0]] for section in (own_section, own_section + 1 - 2 * c)
    ]

    def message(kind, s):
        if kind <= 2:
            ref, target = shard(s, yl, z), (ypeer, zplus, zminus)[kind]
        elif kind <= 4:
            ref, target = shard(s, 1 - yl, z, SPLIT, ROWS - SPLIT), (zplus, zminus)[kind - 3]
        elif kind == 5:
            ref, target = shard(s, yl, z + 3, 0, half), zplus
        elif kind == 6:
            ref, target = shard(s, yl, z + 1, half, half), zminus
        elif kind == 7:
            ref, target = shard(s, yl, z + 2), ypeer
        else:
            ref, target = shard(s, yl, (z + 3, z + 1)[kind - 8], 0, SPLIT), ypeer
        return pltpu.make_async_remote_copy(
            ref, ref, ms_sem.at[kind, s], mr_sem.at[kind, s], device_id=target, device_id_type=MESH
        )

    def load_own(j):
        return pltpu.make_async_copy(a_ref.at[j], abuf.at[0], al_sem.at[0])

    def load_mate(j):
        return pltpu.make_async_copy(a2.at[j], abuf.at[1], al_sem.at[1])

    def keep(s, b):
        return pltpu.make_async_copy(stk.at[b], kept.at[s], k_sem.at[b])

    def swap(s, b, h, tile):
        rows = pl.ds(pl.multiple_of(tile * 256, 256), 256)
        return pltpu.make_async_remote_copy(
            sts.at[b, h, rows], recv.at[s, h, rows], ps_sem.at[b, h, tile], pr_sem.at[s, h, tile],
            device_id=(peer_a, peer_b)[h], device_id_type=MESH,
        )

    def mask_own(s):
        own_column = pl.ds(column(yl, z), 128)
        limit = jnp.where(s % 2 == 0, limits[0], limits[1])
        live = (lax.broadcasted_iota(jnp.int32, (ROWS, 128), 0) < limit).astype(jnp.float32)
        cbuf[s, :, own_column] = (cbuf[s, :, own_column].astype(jnp.float32) * live).astype(jnp.bfloat16)

    own_c(0).start()
    load_own(0).start()
    own_c(0).wait()
    mask_own(0)
    greet((mate, ypeer, zplus, zminus, peer_a, peer_b, peer_y))
    for kind in (0, 1, 2):
        message(kind, 0).start()
    for j in range(SLOTS):
        if j > 0:
            own_c(j).start()
        mate_c(j).start()
    for j in range(SLOTS):
        mate_a(j).start()

    def compute(s, b):
        j = s // 2
        if b == 0:
            mate_a(j).wait_recv()
            load_mate(j).start()
            load_own(j).wait()
        else:
            @pl.when(j < SLOTS - 1)
            def _():
                load_own(j + 1).start()

            load_mate(j).wait()

        @pl.when(j > 0)
        def _():
            keep(s - 2, b).wait()
            for h in range(2):
                for tile in range(2):
                    swap(s - 2, b, h, tile).wait_send()

        @pl.loop(0, 2)
        def _(tile):
            at = pl.multiple_of(tile * 256, 256)
            rows = pl.ds(at, 256)
            for h in range(2):
                block = lax.dot_general(
                    abuf[b, :, pl.ds(h * 512 + at, 256)], cbuf[s],
                    (((0,), (0,)), ((), ())), preferred_element_type=jnp.float32,
                ).astype(jnp.bfloat16)
                if h == 0:
                    sts[b, 0, rows, :] = block[:, 256:768]
                    stk[b, 0, rows, 0:256] = block[:, 0:256]
                    stk[b, 0, rows, 256:512] = block[:, 768:1024]
                else:
                    sts[b, 1, rows, 0:256] = block[:, 768:1024]
                    sts[b, 1, rows, 256:512] = block[:, 512:768]
                    stk[b, 1, rows, :] = block[:, 0:512]
                swap(s, b, h, tile).start()

        keep(s, b).start()

    def tables():
        for h, partner in enumerate((xa, xb)):
            sections = ((x, c), (x, 1 - c), (partner, c), (partner, 1 - c))
            for q, (sx, sc) in enumerate(sections):
                replica, part = section_part(code, (yh * 4 + sx) * 2 + sc)
                low = bounds[replica, part]
                high = bounds[replica, part + 1]

                @pl.loop(0, LAYERS)
                def _(layer):
                    live = (layer >= low) & (layer < high)
                    at = (h * LAYERS + layer) * 4 + q
                    slot_of[at] = jnp.where(live, 2 * (layer - low) + (q % 2), 0) + UNITS * (q // 2)
                    weight_of[at] = jnp.where(live, 1.0, 0.0)

    def early_loads(layer, block, b):
        count = 2 * layer + 2
        rows = pl.ds(pl.multiple_of(block * EROWS, EROWS), EROWS)
        return [
            pltpu.make_async_copy(
                source.at[pl.ds(0, count), h, rows, :], le[b].at[h, pl.ds(g * count, count)], le_sem.at[b, h, g]
            )
            for h in range(2)
            for g, source in enumerate((kept, recv))
        ]

    def early_x(layer, h):
        b = layer % 2
        return pltpu.make_async_remote_copy(
            q2s.at[b, h], q2r.at[layer, h], t2_sem.at[b, h], u2_sem.at[layer, h],
            device_id=(peer_b, peer_a)[h], device_id_type=MESH,
        )

    def early_y(layer, h):
        b = layer % 2
        return pltpu.make_async_remote_copy(
            q3s.at[b, h], peer_sum.at[layer, pl.ds(h * 512, 512), :], t3_sem.at[b, h], u3_sem.at[layer, h],
            device_id=peer_y, device_id_type=MESH,
        )

    def early_store(layer, h):
        b = layer % 2
        return pltpu.make_async_copy(q3k.at[b, h], own_sum.at[layer, pl.ds(h * 512, 512), :], v_sem.at[b, h])

    def early_first(layer):
        p = layer % 2
        count = 2 * layer + 2
        for s in (2 * layer, 2 * layer + 1):
            for h in range(2):
                for tile in range(2):
                    swap(s, 0, h, tile).wait_recv()
        if layer >= 2:
            for h in range(2):
                early_x(layer - 2, h).wait_send()
        for load in early_loads(layer, 0, 0):
            load.start()

        @pl.loop(0, 512 // EROWS // 2)
        def _(pair):
            for b in range(2):
                block = pair * 2 + b

                @pl.when(block + 1 < 512 // EROWS)
                def _():
                    for load in early_loads(layer, block + 1, 1 - b):
                        load.start()

                for load in early_loads(layer, block, b):
                    load.wait()
                rows = pl.ds(pl.multiple_of(block * EROWS, EROWS), EROWS)
                for h in range(2):
                    total = None
                    for q in range(4):
                        at = (h * LAYERS + layer) * 4 + q
                        slot = slot_of[at] + (q // 2) * (count - UNITS)
                        term = le[b][h, slot].astype(jnp.float32) * weight_of[at]
                        total = term if total is None else total + term
                    q2k[p, h, rows, :] = total[:, 0:256]
                    q2s[p, h, rows, :] = total[:, 256:512].astype(jnp.bfloat16)

        for h in range(2):
            early_x(layer, h).start()

    def early_second(layer):
        p = layer % 2
        for h in range(2):
            if layer >= 2:
                early_y(layer - 2, h).wait_send()
                early_store(layer - 2, h).wait()
            early_x(layer, h).wait_recv()

            @pl.loop(0, 512 // EROWS)
            def _(block):
                rows = pl.ds(pl.multiple_of(block * EROWS, EROWS), EROWS)
                total = q2k[p, h, rows, :] + q2r[layer, h, rows, :].astype(jnp.float32)
                q3k[p, h, rows, :] = total[:, 0:128]
                q3s[p, h, rows, :] = total[:, 128:256].astype(jnp.bfloat16)

            early_y(layer, h).start()
            early_store(layer, h).start()

    @pl.loop(0, UNITS + 1)
    def _(it):
        @pl.when(it >= 1)
        def _():
            message(5, it - 1).wait_recv()
            message(6, it - 1).wait_recv()
            message(7, it - 1).start()

        pl.when(it == 1)(tables)
        for layer in range(EARLY):
            pl.when(it == 2 * layer + 5)(functools.partial(early_first, layer))
            if layer < EARLY - 1:
                pl.when(it == 2 * layer + 7)(functools.partial(early_second, layer))

        @pl.when(it < UNITS)
        def _():
            message(0, it).wait_recv()
            message(3, it).start()
            message(4, it).start()
            message(1, it).wait_recv()
            message(5, it).start()
            message(8, it).start()
            message(2, it).wait_recv()
            message(6, it).start()
            message(9, it).start()

        @pl.when(it + 1 < UNITS)
        def _():
            n = it + 1

            @pl.when(n % 2 == 0)
            def _():
                own_c(n // 2).wait()

            @pl.when(n % 2 == 1)
            def _():
                mate_c(n // 2).wait_recv()

            mask_own(n)
            for kind in (0, 1, 2):
                message(kind, n).start()

        @pl.when(it >= 1)
        def _():
            s = it - 1
            for kind in (3, 4, 7, 8, 9):
                message(kind, s).wait_recv()

            @pl.when(s % 2 == 0)
            def _():
                compute(s, 0)

            @pl.when(s % 2 == 1)
            def _():
                compute(s, 1)

    for b in range(2):
        keep(UNITS - 2 + b, b).wait()

    def arrived(tile):
        for s in range(2 * EARLY, UNITS):
            for h in range(2):
                swap(s, 0, h, tile).wait_recv()

    def loads(n, b):
        rows = pl.ds(pl.multiple_of(n * CROWS, CROWS), CROWS)
        return [
            pltpu.make_async_copy(source.at[:, h, rows, :], ld[b].at[h, pl.ds(g * UNITS, UNITS)], ld_sem.at[b, h, g])
            for h in range(2)
            for g, source in enumerate((kept, recv))
        ]

    def send_x(n, b, h):
        return pltpu.make_async_remote_copy(
            p2s.at[b, h], p2r.at[n, h], s2_sem.at[b, h], r2_sem.at[n, h],
            device_id=(peer_b, peer_a)[h], device_id_type=MESH,
        )

    def send_y(n, b, h):
        rows = pl.ds(pl.multiple_of(h * 512 + n * CROWS, CROWS), CROWS)
        return pltpu.make_async_remote_copy(
            p3s.at[b, h], peer_sum.at[pl.ds(EARLY, LATE), rows, :], s3_sem.at[b, h], r3_sem.at[n, h],
            device_id=peer_y, device_id_type=MESH,
        )

    def store(n, b, h):
        return pltpu.make_async_copy(
            p3k.at[b, h], own_sum.at[pl.ds(EARLY, LATE), pl.ds(pl.multiple_of(h * 512 + n * CROWS, CROWS), CROWS), :], o_sem.at[b, h]
        )

    def first(n, b):
        if b == 0:
            @pl.when(n == 0)
            def _():
                arrived(0)
                for load in loads(0, 0):
                    load.start()

        if b == (CHUNKS // 2 - 1) % BUFFERS:
            @pl.when(n == CHUNKS // 2 - 1)
            def _():
                arrived(1)

        @pl.when(n + 1 < CHUNKS)
        def _():
            for load in loads(n + 1, 1 - b % 2):
                load.start()

        for load in loads(n, b % 2):
            load.wait()
        for h in range(2):
            @pl.when(n >= BUFFERS)
            def _():
                send_x(n - BUFFERS, b, h).wait_send()

            @pl.loop(0, LATE)
            def _(layer):
                total = None
                for q in range(4):
                    at = (h * LAYERS + EARLY + layer) * 4 + q
                    term = ld[b % 2][h, slot_of[at]].astype(jnp.float32) * weight_of[at]
                    total = term if total is None else total + term
                p2k[b, h, layer] = total[:, 0:256]
                p2s[b, h, layer] = total[:, 256:512].astype(jnp.bfloat16)

            send_x(n, b, h).start()

    def second(n, b):
        d = b % 2

        @pl.when(n >= 2)
        def _():
            for h in range(2):
                send_y(n - 2, d, h).wait_send()
                store(n - 2, d, h).wait()

        for h in range(2):
            send_x(n, b, h).wait_recv()

            @pl.loop(0, LATE)
            def _(layer):
                total = p2k[b, h, layer] + p2r[n, h, layer].astype(jnp.float32)
                p3k[d, h, layer] = total[:, 0:128]
                p3s[d, h, layer] = total[:, 128:256].astype(jnp.bfloat16)

            send_y(n, d, h).start()
            store(n, d, h).start()

    @pl.loop(0, CHUNKS // BUFFERS + 1)
    def _(it):
        for b in range(BUFFERS):
            n = it * BUFFERS + b

            @pl.when(n < CHUNKS)
            def _():
                first(n, b)

            if b == 1:
                pl.when(it == 0)(functools.partial(early_second, EARLY - 1))

            @pl.when((n >= DELAY) & (n < CHUNKS + DELAY))
            def _():
                second(n - DELAY, (b - DELAY) % BUFFERS)

    for b in range(BUFFERS):
        for h in range(2):
            send_x(CHUNKS - BUFFERS + b, b, h).wait_send()
    for b in range(2):
        for h in range(2):
            send_y(CHUNKS - 2 + b, b, h).wait_send()
            store(CHUNKS - 2 + b, b, h).wait()

    for b in range(2):
        for h in range(2):
            for tile in range(2):
                swap(UNITS - 2 + b, b, h, tile).wait_send()
    for j in range(SLOTS):
        mate_c(j).wait_send()
        mate_a(j).wait_send()

    for layer in range(EARLY):
        for h in range(2):
            early_y(layer, h).wait_recv()
            if layer >= EARLY - 2:
                early_x(layer, h).wait_send()
                early_y(layer, h).wait_send()
                early_store(layer, h).wait()

    @pl.loop(0, UNITS)
    def _(s):
        for kind in range(10):
            message(kind, s).wait_send()

    @pl.loop(0, CHUNKS)
    def _(n):
        for h in range(2):
            send_y(n, 0, h).wait_recv()


def section_part(code, section):
    value = code[section]
    second = jnp.where(value >= 4, 1, 0)
    third = jnp.where(value >= 9, 1, 0)
    return second + third, value - 4 * second - 5 * third


def per_device(activations, cotangents, section_code, boundaries, micro_counts):
    any_spec = pl.BlockSpec(memory_space=pl.ANY)
    smem_spec = pl.BlockSpec(memory_space=pltpu.SMEM)
    dma = pltpu.SemaphoreType.DMA
    blocks = jax.ShapeDtypeStruct((UNITS, 2, 512, 512), jnp.bfloat16)
    own_sum, peer_sum, _, _, _ = pl.pallas_call(
        gradients,
        name="gradients",
        out_shape=(
            jax.ShapeDtypeStruct((LAYERS, WIDTH, 128), jnp.float32),
            jax.ShapeDtypeStruct((LAYERS, WIDTH, 128), jnp.bfloat16),
            blocks,
            blocks,
            jax.ShapeDtypeStruct((SLOTS, ROWS, WIDTH), jnp.bfloat16),
        ),
        in_specs=[smem_spec] * 3 + [any_spec] * 2,
        out_specs=(any_spec,) * 5,
        scratch_shapes=[
            pltpu.VMEM((UNITS, ROWS, 1024), jnp.bfloat16),
            pltpu.VMEM((2, ROWS, WIDTH), jnp.bfloat16),
            pltpu.VMEM((2, 2, 512, 512), jnp.bfloat16),
            pltpu.VMEM((2, 2, 512, 512), jnp.bfloat16),
            pltpu.VMEM((2, 2 * UNITS, CROWS, 512), jnp.bfloat16),
            pltpu.VMEM((2, 2 * UNITS, CROWS, 512), jnp.bfloat16),
            pltpu.VMEM((BUFFERS, 2, LATE, CROWS, 256), jnp.float32),
            pltpu.VMEM((BUFFERS, 2, LATE, CROWS, 256), jnp.bfloat16),
            pltpu.VMEM((CHUNKS, 2, LATE, CROWS, 256), jnp.bfloat16),
            pltpu.VMEM((2, 2, LATE, CROWS, 128), jnp.float32),
            pltpu.VMEM((2, 2, LATE, CROWS, 128), jnp.bfloat16),
            pltpu.SMEM((2 * LAYERS * 4,), jnp.int32),
            pltpu.SMEM((2 * LAYERS * 4,), jnp.float32),
            pltpu.VMEM((2, 4 * EARLY, EROWS, 512), jnp.bfloat16),
            pltpu.VMEM((2, 4 * EARLY, EROWS, 512), jnp.bfloat16),
            pltpu.VMEM((2, 2, 512, 256), jnp.float32),
            pltpu.VMEM((2, 2, 512, 256), jnp.bfloat16),
            pltpu.VMEM((EARLY, 2, 512, 256), jnp.bfloat16),
            pltpu.VMEM((2, 2, 512, 128), jnp.float32),
            pltpu.VMEM((2, 2, 512, 128), jnp.bfloat16),
            dma((SLOTS,)), dma((SLOTS,)), dma((SLOTS,)), dma((SLOTS,)), dma((SLOTS,)),
            dma((10, UNITS)), dma((10, UNITS)), dma((2,)), dma((2,)), dma((2, 2, 2)), dma((UNITS, 2, 2)),
            dma((2, 2, 2)), dma((BUFFERS, 2)), dma((CHUNKS, 2)), dma((2, 2)), dma((CHUNKS, 2)), dma((2, 2)),
            dma((2, 2, 2)), dma((2, 2)), dma((EARLY, 2)), dma((2, 2)), dma((EARLY, 2)), dma((2, 2)),
        ],
        compiler_params=pltpu.CompilerParams(
            collective_id=0, has_side_effects=True, vmem_limit_bytes=60 << 20
        ),
    )(section_code, boundaries, micro_counts, cotangents[0], activations[0])
    return own_sum + peer_sum.astype(jnp.float32)


def solution(mesh):
    placed = (P("section", None, None, "tp"), P("section", None, None, "tp"), P(), P(), P())
    return jax.shard_map(
        per_device, mesh=mesh, in_specs=placed, out_specs=P(None, "tp", "section"), check_vma=False
    )
```
